512 devices in a mesh: group: 2 (over core), ep: 128 (over z_lo, x, y), tp: 2 (over z_hi).
Axes of the slice: x: 4, y: 4, z: 16 (z_hi: 2, z_lo: 8; z = z_hi * 8 + z_lo), core: 2. Of those that a mesh axis runs over, the one named last changes fastest.
Arguments:
- queries: bfloat16 [512, 4, 128, 576], P(('group', 'ep'), None, 'tp'), may hold values from -60 to 60, as said below
- step_rows: bfloat16 [512, 4, 576], P(('group', 'ep')), may hold values from -6 to 6
- cache: bfloat16 [256, 512, 576], P(('group', 'ep')), may hold values from -6 to 6
- lengths: int32 [256], P(('group', 'ep')), may hold values from 2 to 512, as said below
- outgoing: bfloat16 [65536, 576], P(('group', 'ep')), may hold values from -6 to 6
- crossing: int32 [65536], P(('group', 'ep')), may hold values from 0 to 127, as said below
Outputs:
- attended: bfloat16 [512, 4, 128, 512], P(('group', 'ep'), None, 'tp')
The draws below stay inside these ranges and needn't reach their ends.
Inputs may be any that keep to these rules, and one draw needn't show every extreme that they name: `queries`: query entries. `lengths`: some entry equals 512. `crossing`: split each device's 256 entries into 2 equal runs in order; each run names every decode device index exactly once.
All inputs are finite; a program needn't handle non-finite values.
Results may differ from the reference program's by a relative error of at most 0.0029.
Values may be sent and summed in bfloat16 or wider, within the bound.
No kernel may reach another device: no remote copies, remote signals or barrier semaphores. Data moves between devices by JAX's collectives and lax.ppermute only.
A program may use at most 64 MiB of HBM per device.

```python
import jax
import jax.numpy as jnp
from jax import lax

KV_RANK = 512
HEADS = 128
STEPS = 4
RES_DEV = 1
CACHE_LEN = 512
PROMPT_ROWS = 256
LATENT = 576
SEQS_DEV = 2
LEFT_ROWS = 65536
N_GROUP = 2
N_EP = 128
N_TP = 2


def first_rows(key):
    shape_rows = (N_GROUP * N_EP * RES_DEV, LATENT)
    return jnp.clip(jax.random.normal(jax.random.fold_in(key, 11), shape_rows, jnp.float32), -6.0, 6.0)


def token_rows(key):
    shape_rows = (N_GROUP * N_EP * SEQS_DEV, STEPS, LATENT)
    return jax.random.normal(jax.random.fold_in(key, 12), shape_rows, jnp.float32)


def draw_step_rows(key, part):
    shared = token_rows(key)
    return jnp.clip(shared, -6.0, 6.0).astype(jnp.bfloat16)


def draw_queries(key, part):
    shared = token_rows(key)
    key = jax.random.fold_in(key, 4)
    device_total = N_GROUP * N_EP
    noise = jax.random.normal(key, (device_total * SEQS_DEV, STEPS, HEADS, LATENT), jnp.float32)
    values = noise + 0.12 * shared[:, :, None, :]
    return jnp.clip(values, -60.0, 60.0).astype(jnp.bfloat16)


def draw_cache(key, part):
    leading = first_rows(key)
    key = jax.random.fold_in(key, 3)
    values = jax.random.normal(key, (N_GROUP * N_EP * RES_DEV, CACHE_LEN, LATENT), jnp.float32)
    values = values.at[:, 0, :].set(leading)
    return jnp.clip(values, -6.0, 6.0).astype(jnp.bfloat16)


def draw_lengths(key, part):
    key = jax.random.fold_in(key, 6)
    device_total = N_GROUP * N_EP
    ceilings = jax.random.randint(jax.random.fold_in(key, 1), (device_total, 1), 2, CACHE_LEN + 1)
    extra = jax.random.randint(jax.random.fold_in(key, 2), (device_total, RES_DEV), 0, CACHE_LEN)
    values = 2 + extra % (ceilings - 1)
    entry_total = device_total * RES_DEV
    top_place = jax.random.randint(jax.random.fold_in(key, 3), (), 0, entry_total)
    low_place = (top_place + 1) % entry_total
    flat_values = values.reshape(-1).at[top_place].set(CACHE_LEN).at[low_place].set(2)
    return flat_values.astype(jnp.int32)


def draw_crossing(key, part):
    key = jax.random.fold_in(key, 7)
    run_total = N_GROUP * N_EP * N_TP
    run_rows = PROMPT_ROWS // N_TP
    pattern = jnp.arange(run_rows, dtype=jnp.int32) % N_EP
    run_keys = jax.random.split(key, run_total)

    def shuffle_run(run_key):
        return jax.random.permutation(run_key, pattern)
    shuffled = jax.vmap(shuffle_run)(run_keys)
    return shuffled.reshape(-1).astype(jnp.int32)


def levels(stream_key, shape, pieces, least, largest):
    gain, own = 1.0, jax.random.fold_in(stream_key, 6)
    for dim, parts in pieces:
        steps = jnp.exp(jax.random.uniform(jax.random.fold_in(own, dim), (parts,), jnp.float32, least / len(pieces), largest / len(pieces)))
        gain = gain * jnp.repeat(steps, shape[dim] // parts).reshape([-1 if axis == dim else 1 for axis in range(len(shape))])
    return gain


def centred(own_key, dims, width, bound, cuts=(), kind=jnp.bfloat16):
    values = jax.random.normal(own_key, dims, jnp.float32) * width
    if len(cuts) > 0:
        values = levels(own_key, dims, cuts, -0.22, 0.18) * values
    return jnp.clip(values, min=-bound, max=bound).astype(kind)


def setup_inputs(seed: int = 0) -> dict:
    key_of = jax.random.split(jax.random.key(seed), 7)
    return {
        "queries": draw_queries(jax.random.fold_in(key_of[6], 71), 0),
        "step_rows": draw_step_rows(jax.random.fold_in(key_of[6], 71), 0),
        "cache": draw_cache(jax.random.fold_in(key_of[6], 71), 0),
        "lengths": draw_lengths(jax.random.fold_in(key_of[6], 71), 0),
        "outgoing": centred(key_of[4], (LEFT_ROWS, LATENT), 1.0, 6.0, ((0, 256),)),
        "crossing": draw_crossing(jax.random.fold_in(key_of[6], 71), 0),
    }


score_scale = 192.0 ** -0.5
masked_score = -1.0e30


def attend(query_block, base_keys, base_live, step_keys):
    flat_query = query_block.reshape(STEPS * HEADS, LATENT)
    all_keys = jnp.concatenate([base_keys, step_keys], axis=0)
    scores = jnp.dot(flat_query, all_keys.T, preferred_element_type=jnp.float32) * score_scale
    query_step = jnp.arange(STEPS * HEADS, dtype=jnp.int32)[:, None] // HEADS
    key_step = jnp.arange(STEPS, dtype=jnp.int32)[None, :]
    base_seen = jnp.broadcast_to(base_live[None, :], (STEPS * HEADS, base_keys.shape[0]))
    visible = jnp.concatenate([base_seen, key_step <= query_step], axis=1)
    scores = jnp.where(visible, scores, masked_score)
    peak = jnp.max(scores, axis=1, keepdims=True)
    expo = jnp.exp(scores - peak)
    total = jnp.sum(expo, axis=1, keepdims=True)
    weights = expo.astype(jnp.bfloat16)
    mixed = jnp.dot(weights, all_keys[:, :KV_RANK], preferred_element_type=jnp.float32)
    return (mixed / total).astype(jnp.bfloat16).reshape(STEPS, HEADS, KV_RANK)


def reference(queries, step_rows, cache, lengths, outgoing, crossing):
    device_total = N_GROUP * N_EP
    sent_rows = N_EP * PROMPT_ROWS
    order = jnp.argsort(crossing[:sent_rows], stable=True)
    arrived = outgoing[:sent_rows][order].reshape(N_EP, PROMPT_ROWS, LATENT)
    empty_rows = jnp.zeros((N_EP, PROMPT_ROWS, LATENT), jnp.bfloat16)
    arrived_all = jnp.concatenate([empty_rows, arrived], axis=0)
    dev_queries = queries.reshape(device_total, SEQS_DEV, STEPS, HEADS, LATENT)
    dev_steps = step_rows.reshape(device_total, SEQS_DEV, STEPS, LATENT)
    dev_cache = cache.reshape(device_total, RES_DEV, CACHE_LEN, LATENT)
    dev_lengths = lengths.reshape(device_total, RES_DEV)
    positions = jnp.arange(CACHE_LEN, dtype=jnp.int32)

    def one_device(packed):
        device_index, my_queries, my_steps, my_cache, my_lengths, my_arrived = packed
        outputs = []
        for seq_index in range(RES_DEV):
            live_rows = positions < my_lengths[seq_index]
            outputs.append(attend(my_queries[seq_index], my_cache[seq_index], live_rows, my_steps[seq_index]))
        arrive_live = jnp.broadcast_to(device_index >= N_EP, (PROMPT_ROWS,))
        outputs.append(attend(my_queries[RES_DEV], my_arrived, arrive_live, my_steps[RES_DEV]))
        return jnp.stack(outputs)

    device_ids = jnp.arange(device_total, dtype=jnp.int32)
    result = lax.map(one_device, (device_ids, dev_queries, dev_steps, dev_cache, dev_lengths, arrived_all))
    return result.reshape(N_GROUP * N_EP * SEQS_DEV, STEPS, HEADS, KV_RANK)
```

```python
import jax
import jax.numpy as jnp
from jax import lax
from jax.experimental import pallas as pl
from jax.experimental.pallas import tpu as pltpu
from jax.sharding import Mesh, PartitionSpec as P

KV_RANK = 512
PLANE = 16
LINE = 8

score_scale = 192.0 ** (-0.5)
masked_score = -1e30


def product(left, right, dims):
    return lax.dot_general(left, right, (dims, ((), ())), preferred_element_type=jnp.float32)


def picked(where_one, rows, dims):
    selector = jnp.where(where_one, 1.0, 0.0).astype(jnp.bfloat16)
    return product(selector, rows, dims).astype(jnp.bfloat16)


def pack_kernel(slot_ref, latent_ref, packed_ref):
    count = slot_ref.shape[1]
    rows = lax.broadcasted_iota(jnp.int32, (count, count), 0)
    packed_ref[...] = picked(rows == slot_ref[...], latent_ref[...], ((1,), (1,)))


def attend(query, step_keys, first_step, base_scores, base_mix):
    head_count = query.shape[1]
    query = query.reshape(query.shape[0] * head_count, query.shape[2])
    scores = product(query, step_keys, ((1,), (1,))) * score_scale
    query_step = first_step + lax.broadcasted_iota(jnp.int32, scores.shape, 0) // head_count
    key_step = lax.broadcasted_iota(jnp.int32, scores.shape, 1)
    tail_scores = jnp.where(key_step <= query_step, scores, masked_score)
    base_scores = base_scores(query)
    peak = jnp.maximum(
        jnp.max(base_scores, axis=1, keepdims=True), jnp.max(tail_scores, axis=1, keepdims=True)
    )
    base_expo = jnp.exp(base_scores - peak)
    tail_expo = jnp.exp(tail_scores - peak)
    total = jnp.sum(base_expo, axis=1, keepdims=True) + jnp.sum(tail_expo, axis=1, keepdims=True)
    mixed = base_mix(base_expo.astype(jnp.bfloat16)) + product(
        tail_expo.astype(jnp.bfloat16), step_keys[:, :KV_RANK], ((1,), (0,))
    )
    return (mixed * (1.0 / total)).astype(jnp.bfloat16).reshape(-1, head_count, KV_RANK)


def resident(length, query, step_keys, keys):
    def base_scores(flat_query):
        scores = product(flat_query, keys, ((1,), (0,))) * score_scale
        position = lax.broadcasted_iota(jnp.int32, scores.shape, 1)
        return jnp.where(position < length, scores, masked_score)

    return attend(
        query, step_keys, 0, base_scores, lambda weights: product(weights, keys[:KV_RANK], ((1,), (1,)))
    )


def middle_kernel(length_ref, query_ref, step_ref, cache_ref, moved_ref, first_ref, *part_refs):
    decode = lax.axis_index("group") == 1

    @pl.when(decode)
    def _():
        first_ref[...] = resident(length_ref[0], query_ref[0], step_ref[0], cache_ref[0])

    @pl.when(jnp.logical_not(decode))
    def _():
        count = moved_ref.shape[0]
        rows = lax.broadcasted_iota(jnp.int32, (count, count), 0)
        cols = lax.broadcasted_iota(jnp.int32, (count, count), 1)
        run, plane, ahead = rows % 2, (rows // 2) % PLANE, rows // (2 * PLANE)
        source = (plane * LINE + ahead) * 2 + run
        turned = picked(cols == source, moved_ref[...], ((1,), (0,)))
        step = count // LINE
        for part, part_ref in enumerate(part_refs):
            part_ref[...] = turned[part * step : (part + 1) * step]


def last_kernel(length_ref, query_ref, step_ref, cache_ref, first_ref, *refs):
    part_refs, (out_ref, result, sems) = refs[:LINE], refs[LINE:]
    decode = lax.axis_index("group") == 1

    @pl.when(decode)
    def _():
        pltpu.make_async_copy(first_ref, out_ref.at[0], sems.at[0]).start()

    @pl.when(jnp.logical_not(decode))
    def _():
        result[0] = resident(length_ref[0], query_ref[0], step_ref[0], cache_ref[0])
        pltpu.make_async_copy(result.at[0], out_ref.at[0], sems.at[0]).start()

    keys = jnp.concatenate([ref[...] for ref in part_refs], axis=0)

    def base_scores(flat_query):
        scores = product(flat_query, keys, ((1,), (1,))) * score_scale
        return jnp.where(decode, scores, masked_score)

    half = query_ref.shape[1] // 2
    copies = []
    for part in range(2):
        steps = pl.ds(part * half, half)
        result[1, steps] = attend(
            query_ref[1, steps],
            step_ref[1],
            part * half,
            base_scores,
            lambda weights: product(weights, keys[:, :KV_RANK], ((1,), (0,))),
        )
        copy = pltpu.make_async_copy(
            result.at[1, steps], out_ref.at[1, steps], sems.at[1 + part]
        )
        copy.start()
        copies.append(copy)
    pltpu.make_async_copy(result.at[0], out_ref.at[0], sems.at[0]).wait()
    for copy in copies:
        copy.wait()


vmem = pl.BlockSpec(memory_space=pltpu.VMEM)
smem = pl.BlockSpec(memory_space=pltpu.SMEM)
anywhere = pl.BlockSpec(memory_space=pl.ANY)
params = pltpu.CompilerParams(vmem_limit_bytes=16 << 20)


def step_of(place, ahead):
    if ahead == LINE // 2:
        down = place % LINE >= LINE // 2 or place % 2 == 1
        return -ahead if down else ahead
    return ahead if ahead < LINE // 2 else ahead - LINE


def up_line(rows, ahead):
    line_total, ring = PLANE * LINE * 2, LINE * 2
    pairs = []
    for place in range(ring):
        there = (place + step_of(place, ahead)) % ring
        for plane in range(PLANE):
            source = ((place % LINE) * PLANE + plane) * 2 + place // LINE
            target = ((there % LINE) * PLANE + plane) * 2 + there // LINE
            pairs.append((source, line_total + target))
    return lax.ppermute(rows, ("group", "z", "x", "y", "tp"), pairs)


def shards(queries, step_rows, cache, lengths, outgoing, crossing):
    seq_count, steps_total, head_count, latent_width = queries.shape
    row_total = outgoing.shape[0]
    first_shape = jax.ShapeDtypeStruct((steps_total, head_count, KV_RANK), jnp.bfloat16)
    keys = cache.transpose(0, 2, 1)

    run = jnp.arange(row_total, dtype=jnp.int32) // (row_total // 2)
    ahead = (crossing // PLANE - lax.axis_index("z") + LINE) % LINE
    slots = ((crossing % PLANE) * LINE + ahead) * 2 + run
    packed = pl.pallas_call(
        pack_kernel,
        out_shape=jax.ShapeDtypeStruct((row_total, latent_width), jnp.bfloat16),
        in_specs=[vmem] * 2,
        out_specs=vmem,
        compiler_params=params,
    )(slots.reshape(1, row_total), outgoing.T)
    moved = lax.cond(
        lax.axis_index("group") == 0,
        lambda rows: lax.all_to_all(rows, ("x", "y"), 0, 0, tiled=True),
        lambda rows: rows,
        packed.reshape(PLANE, row_total // PLANE, latent_width),
    )
    first, *parts = pl.pallas_call(
        middle_kernel,
        out_shape=[first_shape]
        + [jax.ShapeDtypeStruct((row_total // LINE, latent_width), jnp.bfloat16)] * LINE,
        in_specs=[smem] + [vmem] * 4,
        out_specs=[vmem] * (1 + LINE),
        compiler_params=params,
    )(lengths, queries, step_rows, keys, moved.reshape(row_total, latent_width))
    arrived = [up_line(parts[ahead], ahead) for ahead in (4, 5, 1, 2, 3, 7, 6, 0)]
    return pl.pallas_call(
        last_kernel,
        out_shape=jax.ShapeDtypeStruct((seq_count,) + first_shape.shape, jnp.bfloat16),
        in_specs=[smem] + [vmem] * (4 + LINE),
        out_specs=anywhere,
        scratch_shapes=[
            pltpu.VMEM((seq_count,) + first_shape.shape, jnp.bfloat16),
            pltpu.SemaphoreType.DMA((3,)),
        ],
        compiler_params=params,
    )(lengths, queries, step_rows, keys, first, *arrived)


def solution(mesh):
    parted = Mesh(mesh.devices.reshape(2, LINE, 4, 4, 2), ("group", "z", "x", "y", "tp"))
    own = ("group", "z", "x", "y")
    placed = (
        P(own, None, "tp", None),
        P(own, None, None),
        P(own, None, None),
        P(own),
        P(own, None),
        P(own),
    )
    return jax.shard_map(
        shards,
        mesh=parted,
        in_specs=placed,
        out_specs=P(own, None, "tp", None),
        check_vma=False,
    )
```

```python
import jax
import jax.numpy as jnp
from jax import lax
from jax.experimental import pallas as pl
from jax.experimental.pallas import tpu as pltpu
from jax.sharding import Mesh, PartitionSpec as P

KV_RANK = 512
PEERS = 32
LINE = 4

score_scale = 192.0 ** (-0.5)
masked_score = -1e30


def product(left, right, dims):
    return lax.dot_general(left, right, (dims, ((), ())), preferred_element_type=jnp.float32)


def picked(where_one, rows, dims):
    selector = jnp.where(where_one, 1.0, 0.0).astype(jnp.bfloat16)
    return product(selector, rows, dims).astype(jnp.bfloat16)


def pack_kernel(slot_ref, latent_ref, packed_ref):
    count = slot_ref.shape[1]
    rows = lax.broadcasted_iota(jnp.int32, (count, count), 0)
    packed_ref[...] = picked(rows == slot_ref[...], latent_ref[...], ((1,), (1,)))


def attend(query, step_keys, first_step, base_scores, base_mix):
    head_count = query.shape[1]
    query = query.reshape(query.shape[0] * head_count, query.shape[2])
    scores = product(query, step_keys, ((1,), (1,))) * score_scale
    query_step = first_step + lax.broadcasted_iota(jnp.int32, scores.shape, 0) // head_count
    key_step = lax.broadcasted_iota(jnp.int32, scores.shape, 1)
    tail_scores = jnp.where(key_step <= query_step, scores, masked_score)
    base_scores = base_scores(query)
    peak = jnp.maximum(
        jnp.max(base_scores, axis=1, keepdims=True), jnp.max(tail_scores, axis=1, keepdims=True)
    )
    base_expo = jnp.exp(base_scores - peak)
    tail_expo = jnp.exp(tail_scores - peak)
    total = jnp.sum(base_expo, axis=1, keepdims=True) + jnp.sum(tail_expo, axis=1, keepdims=True)
    mixed = base_mix(base_expo.astype(jnp.bfloat16)) + product(
        tail_expo.astype(jnp.bfloat16), step_keys[:, :KV_RANK], ((1,), (0,))
    )
    return (mixed * (1.0 / total)).astype(jnp.bfloat16).reshape(-1, head_count, KV_RANK)


def resident(length, query, step_keys, keys):
    def base_scores(flat_query):
        scores = product(flat_query, keys, ((1,), (0,))) * score_scale
        position = lax.broadcasted_iota(jnp.int32, scores.shape, 1)
        return jnp.where(position < length, scores, masked_score)

    return attend(
        query, step_keys, 0, base_scores, lambda weights: product(weights, keys[:KV_RANK], ((1,), (1,)))
    )


def middle_kernel(length_ref, query_ref, step_ref, cache_ref, moved_ref, first_ref, *part_refs):
    decode = lax.axis_index("group") == 1

    @pl.when(decode)
    def _():
        first_ref[...] = resident(length_ref[0], query_ref[0], step_ref[0], cache_ref[0])

    @pl.when(jnp.logical_not(decode))
    def _():
        count = moved_ref.shape[0]
        rows = lax.broadcasted_iota(jnp.int32, (count, count), 0)
        cols = lax.broadcasted_iota(jnp.int32, (count, count), 1)
        run, peer, ahead = rows % 2, (rows // 2) % PEERS, rows // (2 * PEERS)
        source = (peer * LINE + ahead) * 2 + run
        turned = picked(cols == source, moved_ref[...], ((1,), (0,)))
        step = count // LINE
        for part, part_ref in enumerate(part_refs):
            part_ref[...] = turned[part * step : (part + 1) * step]


def last_kernel(length_ref, query_ref, step_ref, cache_ref, first_ref, *refs):
    part_refs, (out_ref, result, sems) = refs[:LINE], refs[LINE:]
    decode = lax.axis_index("group") == 1

    @pl.when(decode)
    def _():
        pltpu.make_async_copy(first_ref, out_ref.at[0], sems.at[0]).start()

    @pl.when(jnp.logical_not(decode))
    def _():
        result[0] = resident(length_ref[0], query_ref[0], step_ref[0], cache_ref[0])
        pltpu.make_async_copy(result.at[0], out_ref.at[0], sems.at[0]).start()

    keys = jnp.concatenate([ref[...] for ref in part_refs], axis=0)

    def base_scores(flat_query):
        scores = product(flat_query, keys, ((1,), (1,))) * score_scale
        return jnp.where(decode, scores, masked_score)

    half = query_ref.shape[1] // 2
    copies = []
    for part in range(2):
        steps = pl.ds(part * half, half)
        result[1, steps] = attend(
            query_ref[1, steps],
            step_ref[1],
            part * half,
            base_scores,
            lambda weights: product(weights, keys[:, :KV_RANK], ((1,), (0,))),
        )
        copy = pltpu.make_async_copy(
            result.at[1, steps], out_ref.at[1, steps], sems.at[1 + part]
        )
        copy.start()
        copies.append(copy)
    pltpu.make_async_copy(result.at[0], out_ref.at[0], sems.at[0]).wait()
    for copy in copies:
        copy.wait()


vmem = pl.BlockSpec(memory_space=pltpu.VMEM)
smem = pl.BlockSpec(memory_space=pltpu.SMEM)
anywhere = pl.BlockSpec(memory_space=pl.ANY)
params = pltpu.CompilerParams(vmem_limit_bytes=16 << 20)


def step_of(place, ahead):
    if ahead == LINE // 2:
        down = place % LINE >= LINE // 2 or place % 2 == 1
        return -ahead if down else ahead
    return ahead if ahead < LINE // 2 else ahead - LINE


def up_line(rows, ahead):
    line_total, ring = PEERS * LINE * 2, LINE * 2
    pairs = []
    for place in range(ring):
        there = (place + step_of(place, ahead)) % ring
        for peer in range(PEERS):
            source = ((place % LINE) * PEERS + peer) * 2 + place // LINE
            target = ((there % LINE) * PEERS + peer) * 2 + there // LINE
            pairs.append((source, line_total + target))
    return lax.ppermute(rows, ("group", "pair", "z", "x", "y", "tp"), pairs)


def shards(queries, step_rows, cache, lengths, outgoing, crossing):
    seq_count, steps_total, head_count, latent_width = queries.shape
    row_total = outgoing.shape[0]
    first_shape = jax.ShapeDtypeStruct((steps_total, head_count, KV_RANK), jnp.bfloat16)
    keys = cache.transpose(0, 2, 1)

    run = jnp.arange(row_total, dtype=jnp.int32) // (row_total // 2)
    ahead = (crossing // PEERS - lax.axis_index("pair") + LINE) % LINE
    slots = ((crossing % PEERS) * LINE + ahead) * 2 + run
    packed = pl.pallas_call(
        pack_kernel,
        out_shape=jax.ShapeDtypeStruct((row_total, latent_width), jnp.bfloat16),
        in_specs=[vmem] * 2,
        out_specs=vmem,
        compiler_params=params,
    )(slots.reshape(1, row_total), outgoing.T)
    moved = lax.cond(
        lax.axis_index("group") == 0,
        lambda rows: lax.all_to_all(rows, ("z", "x", "y"), 0, 0, tiled=True),
        lambda rows: rows,
        packed.reshape(PEERS, row_total // PEERS, latent_width),
    )
    first, *parts = pl.pallas_call(
        middle_kernel,
        out_shape=[first_shape]
        + [jax.ShapeDtypeStruct((row_total // LINE, latent_width), jnp.bfloat16)] * LINE,
        in_specs=[smem] + [vmem] * 4,
        out_specs=[vmem] * (1 + LINE),
        compiler_params=params,
    )(lengths, queries, step_rows, keys, moved.reshape(row_total, latent_width))
    arrived = [up_line(parts[ahead], ahead) for ahead in (1, 2, 3, 0)]
    return pl.pallas_call(
        last_kernel,
        out_shape=jax.ShapeDtypeStruct((seq_count,) + first_shape.shape, jnp.bfloat16),
        in_specs=[smem] + [vmem] * (4 + LINE),
        out_specs=anywhere,
        scratch_shapes=[
            pltpu.VMEM((seq_count,) + first_shape.shape, jnp.bfloat16),
            pltpu.SemaphoreType.DMA((3,)),
        ],
        compiler_params=params,
    )(lengths, queries, step_rows, keys, first, *arrived)


def solution(mesh):
    axes = ("group", "pair", "z", "x", "y", "tp")
    parted = Mesh(mesh.devices.reshape(2, LINE, 2, 4, 4, 2), axes)
    own = axes[:-1]
    placed = (
        P(own, None, "tp", None),
        P(own, None, None),
        P(own, None, None),
        P(own),
        P(own, None),
        P(own),
    )
    return jax.shard_map(
        shards,
        mesh=parted,
        in_specs=placed,
        out_specs=P(own, None, "tp", None),
        check_vma=False,
    )
```

```python
import jax
import jax.numpy as jnp
from jax import lax
from jax.experimental import pallas as pl
from jax.experimental.pallas import tpu as pltpu
from jax.sharding import Mesh, PartitionSpec as P

KV_RANK = 512
PEERS = 32
LINE = 4
AHEAD = (1, 0, 2, 3)

score_scale = 192.0 ** (-0.5)
masked_score = -1e30


def product(left, right, dims):
    return lax.dot_general(left, right, (dims, ((), ())), preferred_element_type=jnp.float32)


def picked(where_one, rows, dims):
    selector = jnp.where(where_one, 1.0, 0.0).astype(jnp.bfloat16)
    return product(selector, rows, dims).astype(jnp.bfloat16)


def pack_kernel(slot_ref, latent_ref, packed_ref):
    count = slot_ref.shape[1]
    rows = lax.broadcasted_iota(jnp.int32, (count, count), 0)
    packed_ref[...] = picked(rows == slot_ref[...], latent_ref[...], ((1,), (1,)))


def flat_rows(query_ref, seq):
    query = query_ref[seq]
    return query.reshape(query.shape[0] * query.shape[1], query.shape[2])


def step_scores(query, step_keys, head_count):
    scores = product(query, step_keys, ((1,), (1,))) * score_scale
    query_step = lax.broadcasted_iota(jnp.int32, scores.shape, 0) // head_count
    key_step = lax.broadcasted_iota(jnp.int32, scores.shape, 1)
    return jnp.where(key_step <= query_step, scores, masked_score)


def resident(length, query, step_keys, keys):
    head_count = query.shape[0] // step_keys.shape[0]
    scores = product(query, keys, ((1,), (0,))) * score_scale
    position = lax.broadcasted_iota(jnp.int32, scores.shape, 1)
    base_scores = jnp.where(position < length, scores, masked_score)
    tail_scores = step_scores(query, step_keys, head_count)
    peak = jnp.maximum(
        jnp.max(base_scores, axis=1, keepdims=True), jnp.max(tail_scores, axis=1, keepdims=True)
    )
    base_expo = jnp.exp(base_scores - peak)
    tail_expo = jnp.exp(tail_scores - peak)
    total = jnp.sum(base_expo, axis=1, keepdims=True) + jnp.sum(tail_expo, axis=1, keepdims=True)
    mixed = product(base_expo.astype(jnp.bfloat16), keys[:KV_RANK], ((1,), (1,))) + product(
        tail_expo.astype(jnp.bfloat16), step_keys[:, :KV_RANK], ((1,), (0,))
    )
    return (mixed * (1.0 / total)).astype(jnp.bfloat16).reshape(-1, head_count, KV_RANK)


def steps_only(query, step_keys):
    head_count = query.shape[0] // step_keys.shape[0]
    scores = step_scores(query, step_keys, head_count)
    expo = jnp.exp(scores - jnp.max(scores, axis=1, keepdims=True))
    total = jnp.sum(expo, axis=1, keepdims=True)
    mixed = product(expo.astype(jnp.bfloat16), step_keys[:, :KV_RANK], ((1,), (0,)))
    return (mixed * (1.0 / total)).astype(jnp.bfloat16).reshape(-1, head_count, KV_RANK)


def arrived_and_steps(query_t, keys, base_count, head_count):
    scores = product(keys, query_t, ((1,), (0,))) * score_scale
    step = lax.broadcasted_iota(jnp.int32, scores.shape, 0) - base_count
    query_step = lax.broadcasted_iota(jnp.int32, scores.shape, 1) // head_count
    scores = jnp.where(step <= query_step, scores, masked_score)
    expo = jnp.exp(scores - jnp.max(scores, axis=0, keepdims=True))
    total = jnp.sum(expo, axis=0, keepdims=True)
    mixed = product(expo.astype(jnp.bfloat16), keys[:, :KV_RANK], ((0,), (0,)))
    share = jnp.transpose(jnp.broadcast_to(1.0 / total, (8, total.shape[1])))[:, :1]
    return (mixed * share).astype(jnp.bfloat16).reshape(-1, head_count, KV_RANK)


def middle_kernel(
    length_ref, query_ref, step_ref, cache_ref, moved_ref, first_ref, query_t_ref, tail_ref, *part_refs
):
    decode = lax.axis_index("group") == 1

    @pl.when(decode)
    def _():
        first_ref[...] = resident(length_ref[0], flat_rows(query_ref, 0), step_ref[0], cache_ref[0])
        query_t_ref[...] = jnp.transpose(flat_rows(query_ref, 1))
        tail_ref[...] = jnp.zeros_like(tail_ref)
        tail_ref[: step_ref.shape[1]] = step_ref[1]

    @pl.when(jnp.logical_not(decode))
    def _():
        count = moved_ref.shape[0]
        rows = lax.broadcasted_iota(jnp.int32, (count, count), 0)
        cols = lax.broadcasted_iota(jnp.int32, (count, count), 1)
        run, peer, part = rows % 2, (rows // 2) % PEERS, rows // (2 * PEERS)
        ahead = jnp.zeros_like(part)
        for index, part_ahead in enumerate(AHEAD):
            ahead = jnp.where(part == index, part_ahead, ahead)
        source = (peer * LINE + ahead) * 2 + run
        turned = picked(cols == source, moved_ref[...], ((1,), (0,)))
        step = count // LINE
        for part, part_ref in enumerate(part_refs):
            part_ref[...] = turned[part * step : (part + 1) * step]


def last_kernel(
    length_ref, query_ref, step_ref, cache_ref, first_ref, query_t_ref, tail_ref, *refs
):
    part_refs, (out_ref, result, sems) = refs[:LINE], refs[LINE:]
    decode = lax.axis_index("group") == 1

    @pl.when(decode)
    def _():
        before = pltpu.make_async_copy(first_ref, out_ref.at[0], sems.at[0])
        before.start()
        keys = jnp.concatenate([ref[...] for ref in part_refs] + [tail_ref[...]], axis=0)
        base_count = keys.shape[0] - tail_ref.shape[0]
        result[1] = arrived_and_steps(query_t_ref[...], keys, base_count, query_ref.shape[2])
        after = pltpu.make_async_copy(result.at[1], out_ref.at[1], sems.at[1])
        after.start()
        before.wait()
        after.wait()

    @pl.when(jnp.logical_not(decode))
    def _():
        result[0] = resident(length_ref[0], flat_rows(query_ref, 0), step_ref[0], cache_ref[0])
        before = pltpu.make_async_copy(result.at[0], out_ref.at[0], sems.at[0])
        before.start()
        result[1] = steps_only(flat_rows(query_ref, 1), step_ref[1])
        after = pltpu.make_async_copy(result.at[1], out_ref.at[1], sems.at[1])
        after.start()
        before.wait()
        after.wait()


vmem = pl.BlockSpec(memory_space=pltpu.VMEM)
smem = pl.BlockSpec(memory_space=pltpu.SMEM)
anywhere = pl.BlockSpec(memory_space=pl.ANY)
params = pltpu.CompilerParams(vmem_limit_bytes=16 << 20)


def step_of(place, ahead):
    if ahead == LINE // 2:
        down = place % LINE >= LINE // 2 or place % 2 == 1
        return -ahead if down else ahead
    return ahead if ahead < LINE // 2 else ahead - LINE


def along_line(rows, ahead):
    line_total, ring = PEERS * LINE * 2, LINE * 2
    pairs = []
    for place in range(ring):
        there = (place + step_of(place, ahead)) % ring
        for peer in range(PEERS):
            source = ((place % LINE) * PEERS + peer) * 2 + place // LINE
            target = ((there % LINE) * PEERS + peer) * 2 + there // LINE
            pairs.append((source, line_total + target))
    return lax.ppermute(rows, ("group", "pair", "z", "x", "y", "tp"), pairs)


def shards(queries, step_rows, cache, lengths, outgoing, crossing):
    seq_count, steps_total, head_count, latent_width = queries.shape
    row_total = outgoing.shape[0]
    first_shape = jax.ShapeDtypeStruct((steps_total, head_count, KV_RANK), jnp.bfloat16)
    keys = cache.transpose(0, 2, 1)

    query_rows = steps_total * head_count
    run = jnp.arange(row_total, dtype=jnp.int32) // (row_total // 2)
    ahead = (crossing // PEERS - lax.axis_index("pair") + LINE) % LINE
    slots = ((crossing % PEERS) * LINE + ahead) * 2 + run
    mine = jnp.where(lax.axis_index("group") == 0, outgoing.T, jnp.zeros((), outgoing.dtype))
    packed = pl.pallas_call(
        pack_kernel,
        out_shape=jax.ShapeDtypeStruct((row_total, latent_width), jnp.bfloat16),
        in_specs=[vmem] * 2,
        out_specs=vmem,
        compiler_params=params,
    )(slots.reshape(1, row_total), mine)
    moved = lax.cond(
        lax.axis_index("group") == 0,
        lambda rows: lax.all_to_all(rows, ("z", "x", "y"), 0, 0, tiled=True),
        lambda rows: rows,
        packed.reshape(PEERS, row_total // PEERS, latent_width),
    )
    first, query_t, tail, *parts = pl.pallas_call(
        middle_kernel,
        out_shape=[
            first_shape,
            jax.ShapeDtypeStruct((latent_width, query_rows), jnp.bfloat16),
            jax.ShapeDtypeStruct((16, latent_width), jnp.bfloat16),
        ]
        + [jax.ShapeDtypeStruct((row_total // LINE, latent_width), jnp.bfloat16)] * LINE,
        in_specs=[smem] + [vmem] * 4,
        out_specs=[vmem] * (3 + LINE),
        compiler_params=params,
    )(lengths, queries, step_rows, keys, moved.reshape(row_total, latent_width))
    arrived = [along_line(part, ahead) for part, ahead in zip(parts, AHEAD)]
    return pl.pallas_call(
        last_kernel,
        out_shape=jax.ShapeDtypeStruct((seq_count,) + first_shape.shape, jnp.bfloat16),
        in_specs=[smem] + [vmem] * (6 + LINE),
        out_specs=anywhere,
        scratch_shapes=[
            pltpu.VMEM((seq_count,) + first_shape.shape, jnp.bfloat16),
            pltpu.SemaphoreType.DMA((2,)),
        ],
        compiler_params=params,
    )(lengths, queries, step_rows, keys, first, query_t, tail, *arrived)


def solution(mesh):
    axes = ("group", "pair", "z", "x", "y", "tp")
    parted = Mesh(mesh.devices.reshape(2, LINE, 2, 4, 4, 2), axes)
    own = axes[:-1]
    placed = (
        P(own, None, "tp", None),
        P(own, None, None),
        P(own, None, None),
        P(own),
        P(own, None),
        P(own),
    )
    return jax.shard_map(
        shards,
        mesh=parted,
        in_specs=placed,
        out_specs=P(own, None, "tp", None),
        check_vma=False,
    )
```

```python
import jax
import jax.numpy as jnp
from jax import lax
from jax.experimental import pallas as pl
from jax.experimental.pallas import tpu as pltpu
from jax.sharding import Mesh, PartitionSpec as P

KV_RANK = 512
PEERS = 32
LINE = 4
AHEAD = (1, 2, 3, 0)

score_scale = 192.0 ** (-0.5)
masked_score = -1e30


def product(left, right, dims):
    return lax.dot_general(left, right, (dims, ((), ())), preferred_element_type=jnp.float32)


def picked(where_one, rows, dims):
    selector = jnp.where(where_one, 1.0, 0.0).astype(jnp.bfloat16)
    return product(selector, rows, dims).astype(jnp.bfloat16)


def pack_kernel(slot_ref, latent_ref, packed_ref):
    count = slot_ref.shape[1]
    rows = lax.broadcasted_iota(jnp.int32, (count, count), 0)
    packed_ref[...] = picked(rows == slot_ref[...], latent_ref[...], ((1,), (1,)))


def flat_rows(query_ref, seq):
    query = query_ref[seq]
    return query.reshape(query.shape[0] * query.shape[1], query.shape[2])


def step_scores(query, step_keys, head_count):
    scores = product(query, step_keys, ((1,), (1,))) * score_scale
    query_step = lax.broadcasted_iota(jnp.int32, scores.shape, 0) // head_count
    key_step = lax.broadcasted_iota(jnp.int32, scores.shape, 1)
    return jnp.where(key_step <= query_step, scores, masked_score)


def resident(length, query, step_keys, keys):
    head_count = query.shape[0] // step_keys.shape[0]
    scores = product(query, keys, ((1,), (0,))) * score_scale
    position = lax.broadcasted_iota(jnp.int32, scores.shape, 1)
    base_scores = jnp.where(position < length, scores, masked_score)
    tail_scores = step_scores(query, step_keys, head_count)
    peak = jnp.maximum(
        jnp.max(base_scores, axis=1, keepdims=True), jnp.max(tail_scores, axis=1, keepdims=True)
    )
    base_expo = jnp.exp(base_scores - peak)
    tail_expo = jnp.exp(tail_scores - peak)
    total = jnp.sum(base_expo, axis=1, keepdims=True) + jnp.sum(tail_expo, axis=1, keepdims=True)
    mixed = product(base_expo.astype(jnp.bfloat16), keys[:KV_RANK], ((1,), (1,))) + product(
        tail_expo.astype(jnp.bfloat16), step_keys[:, :KV_RANK], ((1,), (0,))
    )
    return (mixed * (1.0 / total)).astype(jnp.bfloat16).reshape(-1, head_count, KV_RANK)


def steps_only(query, step_keys):
    head_count = query.shape[0] // step_keys.shape[0]
    scores = step_scores(query, step_keys, head_count)
    expo = jnp.exp(scores - jnp.max(scores, axis=1, keepdims=True))
    total = jnp.sum(expo, axis=1, keepdims=True)
    mixed = product(expo.astype(jnp.bfloat16), step_keys[:, :KV_RANK], ((1,), (0,)))
    return (mixed * (1.0 / total)).astype(jnp.bfloat16).reshape(-1, head_count, KV_RANK)


def arrived_and_steps(query_t, keys, base_count, head_count):
    scores = product(keys, query_t, ((1,), (0,))) * score_scale
    step = lax.broadcasted_iota(jnp.int32, scores.shape, 0) - base_count
    query_step = lax.broadcasted_iota(jnp.int32, scores.shape, 1) // head_count
    scores = jnp.where(step <= query_step, scores, masked_score)
    expo = jnp.exp(scores - jnp.max(scores, axis=0, keepdims=True))
    total = jnp.sum(expo, axis=0, keepdims=True)
    share = jnp.transpose(jnp.broadcast_to(1.0 / total, (8, total.shape[1])))[:, :1]
    weights = expo.astype(jnp.bfloat16)
    width = 2 * head_count
    for start in range(0, weights.shape[1], width):
        mixed = product(weights[:, start : start + width], keys[:, :KV_RANK], ((0,), (0,)))
        mixed = mixed * share[start : start + width]
        yield mixed.astype(jnp.bfloat16).reshape(-1, head_count, KV_RANK)


def middle_kernel(
    length_ref, query_ref, step_ref, cache_ref, moved_ref, first_ref, query_t_ref, tail_ref, *part_refs
):
    decode = lax.axis_index("group") == 1

    @pl.when(decode)
    def _():
        first_ref[...] = resident(length_ref[...], flat_rows(query_ref, 0), step_ref[0], cache_ref[0])
        query_t_ref[...] = jnp.transpose(flat_rows(query_ref, 1))
        tail_ref[...] = jnp.zeros_like(tail_ref)
        tail_ref[: step_ref.shape[1]] = step_ref[1]

    @pl.when(jnp.logical_not(decode))
    def _():
        count = moved_ref.shape[0]
        rows = lax.broadcasted_iota(jnp.int32, (count, count), 0)
        cols = lax.broadcasted_iota(jnp.int32, (count, count), 1)
        run, peer, part = rows % 2, (rows // 2) % PEERS, rows // (2 * PEERS)
        ahead = jnp.zeros_like(part)
        for index, part_ahead in enumerate(AHEAD):
            ahead = jnp.where(part == index, part_ahead, ahead)
        source = (peer * LINE + ahead) * 2 + run
        turned = picked(cols == source, moved_ref[...], ((1,), (0,)))
        step = count // LINE
        for part, part_ref in enumerate(part_refs):
            part_ref[...] = turned[part * step : (part + 1) * step]


def last_kernel(
    length_ref, query_ref, step_ref, cache_ref, first_ref, query_t_ref, tail_ref, *refs
):
    part_refs, (out_ref, result, sems) = refs[:LINE], refs[LINE:]
    decode = lax.axis_index("group") == 1

    @pl.when(decode)
    def _():
        before = pltpu.make_async_copy(first_ref, out_ref.at[0], sems.at[0])
        before.start()
        keys = jnp.concatenate([ref[...] for ref in part_refs] + [tail_ref[...]], axis=0)
        base_count = keys.shape[0] - tail_ref.shape[0]
        copies = [before]
        for part, attended in enumerate(
            arrived_and_steps(query_t_ref[...], keys, base_count, query_ref.shape[2])
        ):
            steps = pl.ds(part * attended.shape[0], attended.shape[0])
            result[1, steps] = attended
            copies.append(
                pltpu.make_async_copy(result.at[1, steps], out_ref.at[1, steps], sems.at[1 + part])
            )
            copies[-1].start()
        for copy in copies:
            copy.wait()

    @pl.when(jnp.logical_not(decode))
    def _():
        result[0] = resident(length_ref[...], flat_rows(query_ref, 0), step_ref[0], cache_ref[0])
        before = pltpu.make_async_copy(result.at[0], out_ref.at[0], sems.at[0])
        before.start()
        result[1] = steps_only(flat_rows(query_ref, 1), step_ref[1])
        after = pltpu.make_async_copy(result.at[1], out_ref.at[1], sems.at[1])
        after.start()
        before.wait()
        after.wait()


vmem = pl.BlockSpec(memory_space=pltpu.VMEM)
anywhere = pl.BlockSpec(memory_space=pl.ANY)
params = pltpu.CompilerParams(vmem_limit_bytes=16 << 20)


def step_of(place, ahead):
    if ahead == LINE // 2:
        down = place % LINE >= LINE // 2 or place % 2 == 1
        return -ahead if down else ahead
    return ahead if ahead < LINE // 2 else ahead - LINE


def along_line(rows, ahead):
    line_total, ring = PEERS * LINE * 2, LINE * 2
    pairs = []
    for place in range(ring):
        there = (place + step_of(place, ahead)) % ring
        for peer in range(PEERS):
            source = ((place % LINE) * PEERS + peer) * 2 + place // LINE
            target = ((there % LINE) * PEERS + peer) * 2 + there // LINE
            pairs.append((source, line_total + target))
    return lax.ppermute(rows, ("group", "pair", "z", "x", "y", "tp"), pairs)


def shards(queries, step_rows, cache, lengths, outgoing, crossing):
    seq_count, steps_total, head_count, latent_width = queries.shape
    row_total = outgoing.shape[0]
    first_shape = jax.ShapeDtypeStruct((steps_total, head_count, KV_RANK), jnp.bfloat16)
    keys = cache.transpose(0, 2, 1)
    length = lengths.reshape(1, 1)

    query_rows = steps_total * head_count
    run = jnp.arange(row_total, dtype=jnp.int32) // (row_total // 2)
    ahead = (crossing // PEERS - lax.axis_index("pair") + LINE) % LINE
    slots = ((crossing % PEERS) * LINE + ahead) * 2 + run
    mine = jnp.where(lax.axis_index("group") == 0, outgoing.T, jnp.zeros((), outgoing.dtype))
    packed = pl.pallas_call(
        pack_kernel,
        out_shape=jax.ShapeDtypeStruct((row_total, latent_width), jnp.bfloat16),
        in_specs=[vmem] * 2,
        out_specs=vmem,
        compiler_params=params,
    )(slots.reshape(1, row_total), mine)
    moved = lax.cond(
        lax.axis_index("group") == 0,
        lambda rows: lax.all_to_all(rows, ("z", "x", "y"), 0, 0, tiled=True),
        lambda rows: rows,
        packed.reshape(PEERS, row_total // PEERS, latent_width),
    )
    first, query_t, tail, *parts = pl.pallas_call(
        middle_kernel,
        out_shape=[
            first_shape,
            jax.ShapeDtypeStruct((latent_width, query_rows), jnp.bfloat16),
            jax.ShapeDtypeStruct((16, latent_width), jnp.bfloat16),
        ]
        + [jax.ShapeDtypeStruct((row_total // LINE, latent_width), jnp.bfloat16)] * LINE,
        in_specs=[vmem] * 5,
        out_specs=[vmem] * (3 + LINE),
        compiler_params=params,
    )(length, queries, step_rows, keys, moved.reshape(row_total, latent_width))
    arrived = [along_line(part, ahead) for part, ahead in zip(parts, AHEAD)]
    return pl.pallas_call(
        last_kernel,
        out_shape=jax.ShapeDtypeStruct((seq_count,) + first_shape.shape, jnp.bfloat16),
        in_specs=[vmem] * (7 + LINE),
        out_specs=anywhere,
        scratch_shapes=[
            pltpu.VMEM((seq_count,) + first_shape.shape, jnp.bfloat16),
            pltpu.SemaphoreType.DMA((3,)),
        ],
        compiler_params=params,
    )(length, queries, step_rows, keys, first, query_t, tail, *arrived)


def solution(mesh):
    axes = ("group", "pair", "z", "x", "y", "tp")
    parted = Mesh(mesh.devices.reshape(2, LINE, 2, 4, 4, 2), axes)
    own = axes[:-1]
    placed = (
        P(own, None, "tp", None),
        P(own, None, None),
        P(own, None, None),
        P(own),
        P(own, None),
        P(own),
    )
    return jax.shard_map(
        shards,
        mesh=parted,
        in_specs=placed,
        out_specs=P(own, None, "tp", None),
        check_vma=False,
    )
```

```python
import jax
import jax.numpy as jnp
from jax import lax
from jax.experimental import pallas as pl
from jax.experimental.pallas import tpu as pltpu
from jax.sharding import Mesh, PartitionSpec as P

KV_RANK = 512
PEERS = 32
lap = 64
LINE = 4
AHEAD = (1, 2, 3, 0)

score_scale = 192.0 ** (-0.5)
masked_score = -1e30


def product(left, right, dims):
    return lax.dot_general(left, right, (dims, ((), ())), preferred_element_type=jnp.float32)


def picked(where_one, rows, dims):
    selector = jnp.where(where_one, 1.0, 0.0).astype(jnp.bfloat16)
    return product(selector, rows, dims).astype(jnp.bfloat16)


def pack_kernel(slot_ref, latent_ref, packed_ref):
    width, count = latent_ref.shape
    each = count // 2
    rows = lax.broadcasted_iota(jnp.int32, (each, each), 0)
    blank = jnp.zeros((lap, each), latent_ref.dtype)
    first = picked(
        rows == slot_ref[:, :each], jnp.concatenate([latent_ref[:, :each], blank]), ((1,), (1,))
    )
    second = picked(
        rows == slot_ref[:, each:], jnp.concatenate([blank, latent_ref[:, each:]]), ((1,), (1,))
    )
    inner = width - lap
    both = jnp.concatenate(
        [first[:, :inner], first[:, inner:] + second[:, : 2 * lap], second[:, 2 * lap :]], axis=1
    )
    packed_ref[...] = both.reshape(packed_ref.shape)


def flat_rows(query_ref, seq):
    query = query_ref[seq]
    return query.reshape(query.shape[0] * query.shape[1], query.shape[2])


def step_scores(query, step_keys, head_count):
    scores = product(query, step_keys, ((1,), (1,))) * score_scale
    query_step = lax.broadcasted_iota(jnp.int32, scores.shape, 0) // head_count
    key_step = lax.broadcasted_iota(jnp.int32, scores.shape, 1)
    return jnp.where(key_step <= query_step, scores, masked_score)


def resident(length, query, step_keys, keys):
    head_count = query.shape[0] // step_keys.shape[0]
    scores = product(query, keys, ((1,), (0,))) * score_scale
    position = lax.broadcasted_iota(jnp.int32, scores.shape, 1)
    base_scores = jnp.where(position < length, scores, masked_score)
    tail_scores = step_scores(query, step_keys, head_count)
    peak = jnp.maximum(
        jnp.max(base_scores, axis=1, keepdims=True), jnp.max(tail_scores, axis=1, keepdims=True)
    )
    base_expo = jnp.exp(base_scores - peak)
    tail_expo = jnp.exp(tail_scores - peak)
    total = jnp.sum(base_expo, axis=1, keepdims=True) + jnp.sum(tail_expo, axis=1, keepdims=True)
    mixed = product(base_expo.astype(jnp.bfloat16), keys[:KV_RANK], ((1,), (1,))) + product(
        tail_expo.astype(jnp.bfloat16), step_keys[:, :KV_RANK], ((1,), (0,))
    )
    return (mixed * (1.0 / total)).astype(jnp.bfloat16).reshape(-1, head_count, KV_RANK)


def steps_only(query, step_keys):
    head_count = query.shape[0] // step_keys.shape[0]
    scores = step_scores(query, step_keys, head_count)
    expo = jnp.exp(scores - jnp.max(scores, axis=1, keepdims=True))
    total = jnp.sum(expo, axis=1, keepdims=True)
    mixed = product(expo.astype(jnp.bfloat16), step_keys[:, :KV_RANK], ((1,), (0,)))
    return (mixed * (1.0 / total)).astype(jnp.bfloat16).reshape(-1, head_count, KV_RANK)


def arrived_and_steps(query_t, keys, base_count, head_count):
    scores = product(keys, query_t, ((1,), (0,))) * score_scale
    step = lax.broadcasted_iota(jnp.int32, scores.shape, 0) - base_count
    query_step = lax.broadcasted_iota(jnp.int32, scores.shape, 1) // head_count
    scores = jnp.where(step <= query_step, scores, masked_score)
    expo = jnp.exp(scores - jnp.max(scores, axis=0, keepdims=True))
    total = jnp.sum(expo, axis=0, keepdims=True)
    share = jnp.transpose(jnp.broadcast_to(1.0 / total, (8, total.shape[1])))[:, :1]
    weights = expo.astype(jnp.bfloat16)
    width = 2 * head_count
    for start in range(0, weights.shape[1], width):
        mixed = product(weights[:, start : start + width], keys[:, :KV_RANK], ((0,), (0,)))
        mixed = mixed * share[start : start + width]
        yield mixed.astype(jnp.bfloat16).reshape(-1, head_count, KV_RANK)


def middle_kernel(
    length_ref, query_ref, step_ref, cache_ref, moved_ref, first_ref, query_t_ref, tail_ref, *part_refs
):
    decode = lax.axis_index("group") == 1

    @pl.when(decode)
    def _():
        first_ref[...] = resident(length_ref[0], flat_rows(query_ref, 0), step_ref[0], cache_ref[0])
        query_t_ref[...] = jnp.transpose(flat_rows(query_ref, 1))
        tail_ref[...] = jnp.zeros_like(tail_ref)
        tail_ref[: step_ref.shape[1]] = step_ref[1]

    @pl.when(jnp.logical_not(decode))
    def _():
        count = moved_ref.shape[0] * moved_ref.shape[1]
        rows = lax.broadcasted_iota(jnp.int32, (count, count), 0)
        cols = lax.broadcasted_iota(jnp.int32, (count, count), 1)
        peer, part = rows % PEERS, rows // PEERS
        ahead = jnp.zeros_like(part)
        for index, part_ahead in enumerate(AHEAD):
            ahead = jnp.where(part == index, part_ahead, ahead)
        moved = moved_ref[...].reshape(count, moved_ref.shape[2])
        turned = picked(cols == peer * LINE + ahead, moved, ((1,), (0,)))
        for part, part_ref in enumerate(part_refs):
            part_ref[...] = turned[part * PEERS : (part + 1) * PEERS]


def last_kernel(
    length_ref, query_ref, step_ref, cache_ref, first_ref, query_t_ref, tail_ref, *refs
):
    part_refs, (out_ref, result, sems) = refs[:LINE], refs[LINE:]
    decode = lax.axis_index("group") == 1

    @pl.when(decode)
    def _():
        before = pltpu.make_async_copy(first_ref, out_ref.at[0], sems.at[0])
        before.start()
        both = jnp.concatenate([ref[...] for ref in part_refs], axis=0)
        width = tail_ref.shape[1]
        keys = jnp.concatenate([both[:, :width], both[:, width:], tail_ref[...]], axis=0)
        base_count = keys.shape[0] - tail_ref.shape[0]
        copies = [before]
        for part, attended in enumerate(
            arrived_and_steps(query_t_ref[...], keys, base_count, query_ref.shape[2])
        ):
            steps = pl.ds(part * attended.shape[0], attended.shape[0])
            result[1, steps] = attended
            copies.append(
                pltpu.make_async_copy(result.at[1, steps], out_ref.at[1, steps], sems.at[1 + part])
            )
            copies[-1].start()
        for copy in copies:
            copy.wait()

    @pl.when(jnp.logical_not(decode))
    def _():
        result[0] = resident(length_ref[0], flat_rows(query_ref, 0), step_ref[0], cache_ref[0])
        before = pltpu.make_async_copy(result.at[0], out_ref.at[0], sems.at[0])
        before.start()
        result[1] = steps_only(flat_rows(query_ref, 1), step_ref[1])
        after = pltpu.make_async_copy(result.at[1], out_ref.at[1], sems.at[1])
        after.start()
        before.wait()
        after.wait()


vmem = pl.BlockSpec(memory_space=pltpu.VMEM)
smem = pl.BlockSpec(memory_space=pltpu.SMEM)
anywhere = pl.BlockSpec(memory_space=pl.ANY)
params = pltpu.CompilerParams(vmem_limit_bytes=16 << 20)


def step_of(place, ahead):
    if ahead == LINE // 2:
        down = place % LINE >= LINE // 2 or place % 2 == 1
        return -ahead if down else ahead
    return ahead if ahead < LINE // 2 else ahead - LINE


def along_line(rows, ahead):
    line_total, ring = PEERS * LINE * 2, LINE * 2
    pairs = []
    for place in range(ring):
        there = (place + step_of(place, ahead)) % ring
        for peer in range(PEERS):
            source = ((place % LINE) * PEERS + peer) * 2 + place // LINE
            target = ((there % LINE) * PEERS + peer) * 2 + there // LINE
            pairs.append((source, line_total + target))
    return lax.ppermute(rows, ("group", "pair", "z", "x", "y", "tp"), pairs)


def shards(queries, step_rows, cache, lengths, outgoing, crossing):
    seq_count, steps_total, head_count, latent_width = queries.shape
    row_total = outgoing.shape[0]
    first_shape = jax.ShapeDtypeStruct((steps_total, head_count, KV_RANK), jnp.bfloat16)
    keys = cache.transpose(0, 2, 1)

    query_rows = steps_total * head_count
    ahead = (crossing // PEERS - lax.axis_index("pair") + LINE) % LINE
    slots = (crossing % PEERS) * LINE + ahead
    mine = jnp.where(lax.axis_index("group") == 0, outgoing.T, jnp.zeros((), outgoing.dtype))
    packed = pl.pallas_call(
        pack_kernel,
        out_shape=jax.ShapeDtypeStruct((PEERS, LINE, 2 * latent_width), jnp.bfloat16),
        in_specs=[vmem] * 2,
        out_specs=vmem,
        compiler_params=params,
    )(slots.reshape(1, row_total), mine)
    moved = lax.cond(
        lax.axis_index("group") == 0,
        lambda rows: lax.all_to_all(rows, ("z", "x", "y"), 0, 0, tiled=True),
        lambda rows: rows,
        packed,
    )
    first, query_t, tail, *parts = pl.pallas_call(
        middle_kernel,
        out_shape=[
            first_shape,
            jax.ShapeDtypeStruct((latent_width, query_rows), jnp.bfloat16),
            jax.ShapeDtypeStruct((16, latent_width), jnp.bfloat16),
        ]
        + [jax.ShapeDtypeStruct((PEERS, 2 * latent_width), jnp.bfloat16)] * LINE,
        in_specs=[smem] + [vmem] * 4,
        out_specs=[vmem] * (3 + LINE),
        compiler_params=params,
    )(lengths, queries, step_rows, keys, moved)
    arrived = [along_line(part, ahead) for part, ahead in zip(parts, AHEAD)]
    return pl.pallas_call(
        last_kernel,
        out_shape=jax.ShapeDtypeStruct((seq_count,) + first_shape.shape, jnp.bfloat16),
        in_specs=[smem] + [vmem] * (6 + LINE),
        out_specs=anywhere,
        scratch_shapes=[
            pltpu.VMEM((seq_count,) + first_shape.shape, jnp.bfloat16),
            pltpu.SemaphoreType.DMA((3,)),
        ],
        compiler_params=params,
    )(lengths, queries, step_rows, keys, first, query_t, tail, *arrived)


def solution(mesh):
    axes = ("group", "pair", "z", "x", "y", "tp")
    parted = Mesh(mesh.devices.reshape(2, LINE, 2, 4, 4, 2), axes)
    own = axes[:-1]
    placed = (
        P(own, None, "tp", None),
        P(own, None, None),
        P(own, None, None),
        P(own),
        P(own, None),
        P(own),
    )
    return jax.shard_map(
        shards,
        mesh=parted,
        in_specs=placed,
        out_specs=P(own, None, "tp", None),
        check_vma=False,
    )
```

```python
import jax
import jax.numpy as jnp
from jax import lax
from jax.experimental import pallas as pl
from jax.experimental.pallas import tpu as pltpu
from jax.sharding import Mesh, PartitionSpec as P

KV_RANK = 512
PEERS = 32
lap = 64
LINE = 4
AHEAD = (1, 2, 3, 0)

score_scale = 192.0 ** (-0.5)
masked_score = -1e30


def product(left, right, dims):
    return lax.dot_general(left, right, (dims, ((), ())), preferred_element_type=jnp.float32)


def picked(where_one, rows, dims):
    selector = jnp.where(where_one, 1.0, 0.0).astype(jnp.bfloat16)
    return product(selector, rows, dims).astype(jnp.bfloat16)


def pack_kernel(slot_ref, latent_ref, packed_ref):
    width, count = latent_ref.shape
    each = count // 2
    rows = lax.broadcasted_iota(jnp.int32, (each, each), 0)
    blank = jnp.zeros((lap, each), latent_ref.dtype)
    first = picked(
        rows == slot_ref[:, :each], jnp.concatenate([latent_ref[:, :each], blank]), ((1,), (1,))
    )
    second = picked(
        rows == slot_ref[:, each:], jnp.concatenate([blank, latent_ref[:, each:]]), ((1,), (1,))
    )
    inner = width - lap
    both = jnp.concatenate(
        [first[:, :inner], first[:, inner:] + second[:, : 2 * lap], second[:, 2 * lap :]], axis=1
    )
    packed_ref[...] = both.reshape(packed_ref.shape)


def flat_rows(query_ref, seq):
    query = query_ref[seq]
    return query.reshape(query.shape[0] * query.shape[1], query.shape[2])


def step_scores(query, step_keys, head_count):
    scores = product(query, step_keys, ((1,), (1,))) * score_scale
    query_step = lax.broadcasted_iota(jnp.int32, scores.shape, 0) // head_count
    key_step = lax.broadcasted_iota(jnp.int32, scores.shape, 1)
    return jnp.where(key_step <= query_step, scores, masked_score)


def resident(length, query, step_keys, keys):
    head_count = query.shape[0] // step_keys.shape[0]
    scores = product(query, keys, ((1,), (0,))) * score_scale
    position = lax.broadcasted_iota(jnp.int32, scores.shape, 1)
    base_scores = jnp.where(position < length, scores, masked_score)
    tail_scores = step_scores(query, step_keys, head_count)
    peak = jnp.maximum(
        jnp.max(base_scores, axis=1, keepdims=True), jnp.max(tail_scores, axis=1, keepdims=True)
    )
    base_expo = jnp.exp(base_scores - peak)
    tail_expo = jnp.exp(tail_scores - peak)
    total = jnp.sum(base_expo, axis=1, keepdims=True) + jnp.sum(tail_expo, axis=1, keepdims=True)
    mixed = product(base_expo.astype(jnp.bfloat16), keys[:KV_RANK], ((1,), (1,))) + product(
        tail_expo.astype(jnp.bfloat16), step_keys[:, :KV_RANK], ((1,), (0,))
    )
    return (mixed * (1.0 / total)).astype(jnp.bfloat16).reshape(-1, head_count, KV_RANK)


def steps_only(query, step_keys):
    head_count = query.shape[0] // step_keys.shape[0]
    scores = step_scores(query, step_keys, head_count)
    expo = jnp.exp(scores - jnp.max(scores, axis=1, keepdims=True))
    total = jnp.sum(expo, axis=1, keepdims=True)
    mixed = product(expo.astype(jnp.bfloat16), step_keys[:, :KV_RANK], ((1,), (0,)))
    return (mixed * (1.0 / total)).astype(jnp.bfloat16).reshape(-1, head_count, KV_RANK)


def arrived_and_steps(query_t, keys, base_count, head_count):
    scores = product(keys, query_t, ((1,), (0,))) * score_scale
    step = lax.broadcasted_iota(jnp.int32, scores.shape, 0) - base_count
    query_step = lax.broadcasted_iota(jnp.int32, scores.shape, 1) // head_count
    scores = jnp.where(step <= query_step, scores, masked_score)
    expo = jnp.exp(scores - jnp.max(scores, axis=0, keepdims=True))
    total = jnp.sum(expo, axis=0, keepdims=True)
    share = jnp.transpose(jnp.broadcast_to(1.0 / total, (8, total.shape[1])))[:, :1]
    weights = expo.astype(jnp.bfloat16)
    width = 2 * head_count
    for start in range(0, weights.shape[1], width):
        mixed = product(weights[:, start : start + width], keys[:, :KV_RANK], ((0,), (0,)))
        mixed = mixed * share[start : start + width]
        yield mixed.astype(jnp.bfloat16).reshape(-1, head_count, KV_RANK)


def resident_kernel(length_ref, query_ref, step_ref, cache_ref, after_ref, first_ref):
    first_ref[...] = resident(length_ref[0], flat_rows(query_ref, 0), step_ref[0], cache_ref[0])


def middle_kernel(query_ref, step_ref, moved_ref, query_t_ref, tail_ref, *part_refs):
    decode = lax.axis_index("group") == 1

    @pl.when(decode)
    def _():
        query_t_ref[...] = jnp.transpose(flat_rows(query_ref, 1))
        tail_ref[...] = jnp.zeros_like(tail_ref)
        tail_ref[: step_ref.shape[1]] = step_ref[1]

    @pl.when(jnp.logical_not(decode))
    def _():
        count = moved_ref.shape[0] * moved_ref.shape[1]
        rows = lax.broadcasted_iota(jnp.int32, (count, count), 0)
        cols = lax.broadcasted_iota(jnp.int32, (count, count), 1)
        peer, part = rows % PEERS, rows // PEERS
        ahead = jnp.zeros_like(part)
        for index, part_ahead in enumerate(AHEAD):
            ahead = jnp.where(part == index, part_ahead, ahead)
        moved = moved_ref[...].reshape(count, moved_ref.shape[2])
        turned = picked(cols == peer * LINE + ahead, moved, ((1,), (0,)))
        for part, part_ref in enumerate(part_refs):
            part_ref[...] = turned[part * PEERS : (part + 1) * PEERS]


def last_kernel(query_ref, step_ref, first_ref, query_t_ref, tail_ref, *refs):
    part_refs, (out_ref, result, sems) = refs[:LINE], refs[LINE:]
    decode = lax.axis_index("group") == 1
    before = pltpu.make_async_copy(first_ref, out_ref.at[0], sems.at[0])
    before.start()

    @pl.when(decode)
    def _():
        both = jnp.concatenate([ref[...] for ref in part_refs], axis=0)
        width = tail_ref.shape[1]
        keys = jnp.concatenate([both[:, :width], both[:, width:], tail_ref[...]], axis=0)
        base_count = keys.shape[0] - tail_ref.shape[0]
        copies = []
        for part, attended in enumerate(
            arrived_and_steps(query_t_ref[...], keys, base_count, query_ref.shape[2])
        ):
            steps = pl.ds(part * attended.shape[0], attended.shape[0])
            result[steps] = attended
            copies.append(
                pltpu.make_async_copy(result.at[steps], out_ref.at[1, steps], sems.at[1 + part])
            )
            copies[-1].start()
        for copy in copies:
            copy.wait()

    @pl.when(jnp.logical_not(decode))
    def _():
        result[...] = steps_only(flat_rows(query_ref, 1), step_ref[1])
        after = pltpu.make_async_copy(result, out_ref.at[1], sems.at[1])
        after.start()
        after.wait()

    before.wait()


vmem = pl.BlockSpec(memory_space=pltpu.VMEM)
smem = pl.BlockSpec(memory_space=pltpu.SMEM)
anywhere = pl.BlockSpec(memory_space=pl.ANY)
params = pltpu.CompilerParams(vmem_limit_bytes=16 << 20)


def step_of(place, ahead):
    if ahead == LINE // 2:
        down = place % LINE >= LINE // 2 or place % 2 == 1
        return -ahead if down else ahead
    return ahead if ahead < LINE // 2 else ahead - LINE


def along_line(rows, ahead):
    line_total, ring = PEERS * LINE * 2, LINE * 2
    pairs = []
    for place in range(ring):
        there = (place + step_of(place, ahead)) % ring
        for peer in range(PEERS):
            source = ((place % LINE) * PEERS + peer) * 2 + place // LINE
            target = ((there % LINE) * PEERS + peer) * 2 + there // LINE
            pairs.append((source, line_total + target))
    return lax.ppermute(rows, ("group", "pair", "z", "x", "y", "tp"), pairs)


def shards(queries, step_rows, cache, lengths, outgoing, crossing):
    seq_count, steps_total, head_count, latent_width = queries.shape
    row_total = outgoing.shape[0]
    first_shape = jax.ShapeDtypeStruct((steps_total, head_count, KV_RANK), jnp.bfloat16)
    keys = cache.transpose(0, 2, 1)

    query_rows = steps_total * head_count
    ahead = (crossing // PEERS - lax.axis_index("pair") + LINE) % LINE
    slots = (crossing % PEERS) * LINE + ahead
    mine = jnp.where(lax.axis_index("group") == 0, outgoing.T, jnp.zeros((), outgoing.dtype))
    packed = pl.pallas_call(
        pack_kernel,
        out_shape=jax.ShapeDtypeStruct((PEERS, LINE, 2 * latent_width), jnp.bfloat16),
        in_specs=[vmem] * 2,
        out_specs=vmem,
        compiler_params=params,
    )(slots.reshape(1, row_total), mine)
    moved = lax.cond(
        lax.axis_index("group") == 0,
        lambda rows: lax.all_to_all(rows, ("z", "x", "y"), 0, 0, tiled=True),
        lambda rows: rows,
        packed,
    )
    query_t, tail, *parts = pl.pallas_call(
        middle_kernel,
        out_shape=[
            jax.ShapeDtypeStruct((latent_width, query_rows), jnp.bfloat16),
            jax.ShapeDtypeStruct((16, latent_width), jnp.bfloat16),
        ]
        + [jax.ShapeDtypeStruct((PEERS, 2 * latent_width), jnp.bfloat16)] * LINE,
        in_specs=[vmem] * 3,
        out_specs=[vmem] * (2 + LINE),
        compiler_params=params,
    )(queries, step_rows, moved)
    arrived = [along_line(part, ahead) for part, ahead in zip(parts, AHEAD)]
    first = pl.pallas_call(
        resident_kernel,
        out_shape=first_shape,
        in_specs=[smem] + [vmem] * 3 + [anywhere],
        out_specs=vmem,
        compiler_params=params,
    )(lengths, queries, step_rows, keys, tail)
    return pl.pallas_call(
        last_kernel,
        out_shape=jax.ShapeDtypeStruct((seq_count,) + first_shape.shape, jnp.bfloat16),
        in_specs=[vmem] * (5 + LINE),
        out_specs=anywhere,
        scratch_shapes=[
            pltpu.VMEM(first_shape.shape, jnp.bfloat16),
            pltpu.SemaphoreType.DMA((3,)),
        ],
        compiler_params=params,
    )(queries, step_rows, first, query_t, tail, *arrived)


def solution(mesh):
    axes = ("group", "pair", "z", "x", "y", "tp")
    parted = Mesh(mesh.devices.reshape(2, LINE, 2, 4, 4, 2), axes)
    own = axes[:-1]
    placed = (
        P(own, None, "tp", None),
        P(own, None, None),
        P(own, None, None),
        P(own),
        P(own, None),
        P(own),
    )
    return jax.shard_map(
        shards,
        mesh=parted,
        in_specs=placed,
        out_specs=P(own, None, "tp", None),
        check_vma=False,
    )
```

```python
import jax
import jax.numpy as jnp
from jax import lax
from jax.experimental import pallas as pl
from jax.experimental.pallas import tpu as pltpu
from jax.sharding import Mesh, PartitionSpec as P

KV_RANK = 512
PEERS = 32
lap = 64
LINE = 4
AHEAD = ((1, 2), (2, 1), (3, 3), (0, 0))

score_scale = 192.0 ** (-0.5)
masked_score = -1e30


def product(left, right, dims):
    return lax.dot_general(left, right, (dims, ((), ())), preferred_element_type=jnp.float32)


def picked(where_one, rows, dims):
    selector = jnp.where(where_one, 1.0, 0.0).astype(jnp.bfloat16)
    return product(selector, rows, dims).astype(jnp.bfloat16)


def pack_kernel(slot_ref, latent_ref, packed_ref):
    width, count = latent_ref.shape
    each = count // 2
    rows = lax.broadcasted_iota(jnp.int32, (each, each), 0)
    blank = jnp.zeros((lap, each), latent_ref.dtype)
    first = picked(
        rows == slot_ref[:, :each], jnp.concatenate([latent_ref[:, :each], blank]), ((1,), (1,))
    )
    second = picked(
        rows == slot_ref[:, each:], jnp.concatenate([blank, latent_ref[:, each:]]), ((1,), (1,))
    )
    inner = width - lap
    both = jnp.concatenate(
        [first[:, :inner], first[:, inner:] + second[:, : 2 * lap], second[:, 2 * lap :]], axis=1
    )
    packed_ref[...] = both.reshape(packed_ref.shape)


def flat_rows(query_ref, seq):
    query = query_ref[seq]
    return query.reshape(query.shape[0] * query.shape[1], query.shape[2])


def step_scores(query, step_keys, head_count):
    scores = product(query, step_keys, ((1,), (1,))) * score_scale
    query_step = lax.broadcasted_iota(jnp.int32, scores.shape, 0) // head_count
    key_step = lax.broadcasted_iota(jnp.int32, scores.shape, 1)
    return jnp.where(key_step <= query_step, scores, masked_score)


def resident(length, query, step_keys, keys):
    head_count = query.shape[0] // step_keys.shape[0]
    scores = product(query, keys, ((1,), (0,))) * score_scale
    position = lax.broadcasted_iota(jnp.int32, scores.shape, 1)
    base_scores = jnp.where(position < length, scores, masked_score)
    tail_scores = step_scores(query, step_keys, head_count)
    peak = jnp.maximum(
        jnp.max(base_scores, axis=1, keepdims=True), jnp.max(tail_scores, axis=1, keepdims=True)
    )
    base_expo = jnp.exp(base_scores - peak)
    tail_expo = jnp.exp(tail_scores - peak)
    total = jnp.sum(base_expo, axis=1, keepdims=True) + jnp.sum(tail_expo, axis=1, keepdims=True)
    mixed = product(base_expo.astype(jnp.bfloat16), keys[:KV_RANK], ((1,), (1,))) + product(
        tail_expo.astype(jnp.bfloat16), step_keys[:, :KV_RANK], ((1,), (0,))
    )
    return (mixed * (1.0 / total)).astype(jnp.bfloat16).reshape(-1, head_count, KV_RANK)


def steps_only(query, step_keys):
    head_count = query.shape[0] // step_keys.shape[0]
    scores = step_scores(query, step_keys, head_count)
    expo = jnp.exp(scores - jnp.max(scores, axis=1, keepdims=True))
    total = jnp.sum(expo, axis=1, keepdims=True)
    mixed = product(expo.astype(jnp.bfloat16), step_keys[:, :KV_RANK], ((1,), (0,)))
    return (mixed * (1.0 / total)).astype(jnp.bfloat16).reshape(-1, head_count, KV_RANK)


def arrived_and_steps(query_t, keys, base_count, head_count):
    scores = product(keys, query_t, ((1,), (0,))) * score_scale
    step = lax.broadcasted_iota(jnp.int32, scores.shape, 0) - base_count
    query_step = lax.broadcasted_iota(jnp.int32, scores.shape, 1) // head_count
    scores = jnp.where(step <= query_step, scores, masked_score)
    expo = jnp.exp(scores - jnp.max(scores, axis=0, keepdims=True))
    total = jnp.sum(expo, axis=0, keepdims=True)
    share = jnp.transpose(jnp.broadcast_to(1.0 / total, (8, total.shape[1])))[:, :1]
    weights = expo.astype(jnp.bfloat16)
    width = 2 * head_count
    for start in range(0, weights.shape[1], width):
        mixed = product(weights[:, start : start + width], keys[:, :KV_RANK], ((0,), (0,)))
        mixed = mixed * share[start : start + width]
        yield mixed.astype(jnp.bfloat16).reshape(-1, head_count, KV_RANK)


def resident_kernel(length_ref, query_ref, step_ref, cache_ref, after_ref, first_ref):
    first_ref[...] = resident(length_ref[0], flat_rows(query_ref, 0), step_ref[0], cache_ref[0])


def middle_kernel(query_ref, step_ref, moved_ref, query_t_ref, tail_ref, *part_refs):
    decode = lax.axis_index("group") == 1

    @pl.when(decode)
    def _():
        query_t_ref[...] = jnp.transpose(flat_rows(query_ref, 1))
        tail_ref[...] = jnp.zeros_like(tail_ref)
        tail_ref[: step_ref.shape[1]] = step_ref[1]

    @pl.when(jnp.logical_not(decode))
    def _():
        count = moved_ref.shape[0] * moved_ref.shape[1]
        rows = lax.broadcasted_iota(jnp.int32, (count, count), 0)
        cols = lax.broadcasted_iota(jnp.int32, (count, count), 1)
        peer, part = rows % PEERS, rows // PEERS
        ahead = jnp.zeros_like(part)
        upper = lax.axis_index("z") == 1
        for index, (low_ahead, high_ahead) in enumerate(AHEAD):
            ahead = jnp.where(part == index, jnp.where(upper, high_ahead, low_ahead), ahead)
        moved = moved_ref[...].reshape(count, moved_ref.shape[2])
        turned = picked(cols == peer * LINE + ahead, moved, ((1,), (0,)))
        for part, part_ref in enumerate(part_refs):
            part_ref[...] = turned[part * PEERS : (part + 1) * PEERS]


def last_kernel(query_ref, step_ref, first_ref, query_t_ref, tail_ref, *refs):
    part_refs, (out_ref, result, sems) = refs[:LINE], refs[LINE:]
    decode = lax.axis_index("group") == 1
    before = pltpu.make_async_copy(first_ref, out_ref.at[0], sems.at[0])
    before.start()

    @pl.when(decode)
    def _():
        both = jnp.concatenate([ref[...] for ref in part_refs], axis=0)
        width = tail_ref.shape[1]
        keys = jnp.concatenate([both[:, :width], both[:, width:], tail_ref[...]], axis=0)
        base_count = keys.shape[0] - tail_ref.shape[0]
        copies = []
        for part, attended in enumerate(
            arrived_and_steps(query_t_ref[...], keys, base_count, query_ref.shape[2])
        ):
            steps = pl.ds(part * attended.shape[0], attended.shape[0])
            result[steps] = attended
            copies.append(
                pltpu.make_async_copy(result.at[steps], out_ref.at[1, steps], sems.at[1 + part])
            )
            copies[-1].start()
        for copy in copies:
            copy.wait()

    @pl.when(jnp.logical_not(decode))
    def _():
        result[...] = steps_only(flat_rows(query_ref, 1), step_ref[1])
        after = pltpu.make_async_copy(result, out_ref.at[1], sems.at[1])
        after.start()
        after.wait()

    before.wait()


vmem = pl.BlockSpec(memory_space=pltpu.VMEM)
smem = pl.BlockSpec(memory_space=pltpu.SMEM)
anywhere = pl.BlockSpec(memory_space=pl.ANY)
params = pltpu.CompilerParams(vmem_limit_bytes=16 << 20)


def step_of(place, ahead):
    if ahead == LINE // 2:
        down = place % LINE >= LINE // 2 or place % 2 == 1
        return -ahead if down else ahead
    return ahead if ahead < LINE // 2 else ahead - LINE


def along_line(rows, index):
    line_total, ring = PEERS * LINE * 2, LINE * 2
    pairs = []
    for place in range(ring):
        for peer in range(PEERS):
            there = (place + step_of(place, AHEAD[index][peer // (PEERS // 2)])) % ring
            source = ((place % LINE) * PEERS + peer) * 2 + place // LINE
            target = ((there % LINE) * PEERS + peer) * 2 + there // LINE
            pairs.append((source, line_total + target))
    return lax.ppermute(rows, ("group", "pair", "z", "x", "y", "tp"), pairs)


def shards(queries, step_rows, cache, lengths, outgoing, crossing):
    seq_count, steps_total, head_count, latent_width = queries.shape
    row_total = outgoing.shape[0]
    first_shape = jax.ShapeDtypeStruct((steps_total, head_count, KV_RANK), jnp.bfloat16)
    keys = cache.transpose(0, 2, 1)

    query_rows = steps_total * head_count
    ahead = (crossing // PEERS - lax.axis_index("pair") + LINE) % LINE
    slots = (crossing % PEERS) * LINE + ahead
    mine = jnp.where(lax.axis_index("group") == 0, outgoing.T, jnp.zeros((), outgoing.dtype))
    packed = pl.pallas_call(
        pack_kernel,
        out_shape=jax.ShapeDtypeStruct((PEERS, LINE, 2 * latent_width), jnp.bfloat16),
        in_specs=[vmem] * 2,
        out_specs=vmem,
        compiler_params=params,
    )(slots.reshape(1, row_total), mine)
    moved = lax.cond(
        lax.axis_index("group") == 0,
        lambda rows: lax.all_to_all(rows, ("z", "x", "y"), 0, 0, tiled=True),
        lambda rows: rows,
        packed,
    )
    query_t, tail, *parts = pl.pallas_call(
        middle_kernel,
        out_shape=[
            jax.ShapeDtypeStruct((latent_width, query_rows), jnp.bfloat16),
            jax.ShapeDtypeStruct((16, latent_width), jnp.bfloat16),
        ]
        + [jax.ShapeDtypeStruct((PEERS, 2 * latent_width), jnp.bfloat16)] * LINE,
        in_specs=[vmem] * 3,
        out_specs=[vmem] * (2 + LINE),
        compiler_params=params,
    )(queries, step_rows, moved)
    arrived = [along_line(part, index) for index, part in enumerate(parts)]
    first = pl.pallas_call(
        resident_kernel,
        out_shape=first_shape,
        in_specs=[smem] + [vmem] * 3 + [anywhere],
        out_specs=vmem,
        compiler_params=params,
    )(lengths, queries, step_rows, keys, tail)
    return pl.pallas_call(
        last_kernel,
        out_shape=jax.ShapeDtypeStruct((seq_count,) + first_shape.shape, jnp.bfloat16),
        in_specs=[vmem] * (5 + LINE),
        out_specs=anywhere,
        scratch_shapes=[
            pltpu.VMEM(first_shape.shape, jnp.bfloat16),
            pltpu.SemaphoreType.DMA((3,)),
        ],
        compiler_params=params,
    )(queries, step_rows, first, query_t, tail, *arrived)


def solution(mesh):
    axes = ("group", "pair", "z", "x", "y", "tp")
    parted = Mesh(mesh.devices.reshape(2, LINE, 2, 4, 4, 2), axes)
    own = axes[:-1]
    placed = (
        P(own, None, "tp", None),
        P(own, None, None),
        P(own, None, None),
        P(own),
        P(own, None),
        P(own),
    )
    return jax.shard_map(
        shards,
        mesh=parted,
        in_specs=placed,
        out_specs=P(own, None, "tp", None),
        check_vma=False,
    )
```

```python
import jax
import jax.numpy as jnp
from jax import lax
from jax.experimental import pallas as pl
from jax.experimental.pallas import tpu as pltpu
from jax.sharding import Mesh, PartitionSpec as P

KV_RANK = 512
PEERS = 32
lap = 64
LINE = 4
AHEAD = ((1, 2), (2, 1), (3, 3), (0, 0))

score_scale = 192.0 ** (-0.5)
masked_score = -1e30


def product(left, right, dims):
    return lax.dot_general(left, right, (dims, ((), ())), preferred_element_type=jnp.float32)


def picked(where_one, rows, dims):
    selector = jnp.where(where_one, 1.0, 0.0).astype(jnp.bfloat16)
    return product(selector, rows, dims).astype(jnp.bfloat16)


def pack_kernel(slot_ref, latent_ref, packed_ref):
    width, count = latent_ref.shape
    each = count // 2
    rows = lax.broadcasted_iota(jnp.int32, (each, each), 0)
    blank = jnp.zeros((lap, each), latent_ref.dtype)
    first = picked(
        rows == slot_ref[:, :each], jnp.concatenate([latent_ref[:, :each], blank]), ((1,), (1,))
    )
    second = picked(
        rows == slot_ref[:, each:], jnp.concatenate([blank, latent_ref[:, each:]]), ((1,), (1,))
    )
    inner = width - lap
    both = jnp.concatenate(
        [first[:, :inner], first[:, inner:] + second[:, : 2 * lap], second[:, 2 * lap :]], axis=1
    )
    packed_ref[...] = both.reshape(packed_ref.shape)


def flat_rows(query_ref, seq):
    query = query_ref[seq]
    return query.reshape(query.shape[0] * query.shape[1], query.shape[2])


def step_scores(query, step_keys, head_count):
    scores = product(query, step_keys, ((1,), (1,))) * score_scale
    query_step = lax.broadcasted_iota(jnp.int32, scores.shape, 0) // head_count
    key_step = lax.broadcasted_iota(jnp.int32, scores.shape, 1)
    return jnp.where(key_step <= query_step, scores, masked_score)


def resident(length, query, step_keys, keys):
    head_count = query.shape[0] // step_keys.shape[0]
    scores = product(query, keys, ((1,), (0,))) * score_scale
    position = lax.broadcasted_iota(jnp.int32, scores.shape, 1)
    base_scores = jnp.where(position < length, scores, masked_score)
    tail_scores = step_scores(query, step_keys, head_count)
    peak = jnp.maximum(
        jnp.max(base_scores, axis=1, keepdims=True), jnp.max(tail_scores, axis=1, keepdims=True)
    )
    base_expo = jnp.exp(base_scores - peak)
    tail_expo = jnp.exp(tail_scores - peak)
    total = jnp.sum(base_expo, axis=1, keepdims=True) + jnp.sum(tail_expo, axis=1, keepdims=True)
    mixed = product(base_expo.astype(jnp.bfloat16), keys[:KV_RANK], ((1,), (1,))) + product(
        tail_expo.astype(jnp.bfloat16), step_keys[:, :KV_RANK], ((1,), (0,))
    )
    return (mixed * (1.0 / total)).astype(jnp.bfloat16).reshape(-1, head_count, KV_RANK)


def steps_only(query, step_keys):
    head_count = query.shape[0] // step_keys.shape[0]
    scores = step_scores(query, step_keys, head_count)
    expo = jnp.exp(scores - jnp.max(scores, axis=1, keepdims=True))
    total = jnp.sum(expo, axis=1, keepdims=True)
    mixed = product(expo.astype(jnp.bfloat16), step_keys[:, :KV_RANK], ((1,), (0,)))
    return (mixed * (1.0 / total)).astype(jnp.bfloat16).reshape(-1, head_count, KV_RANK)


def arrived_and_steps(query_t, keys, base_count, head_count):
    scores = product(keys, query_t, ((1,), (0,))) * score_scale
    step = lax.broadcasted_iota(jnp.int32, scores.shape, 0) - base_count
    query_step = lax.broadcasted_iota(jnp.int32, scores.shape, 1) // head_count
    scores = jnp.where(step <= query_step, scores, masked_score)
    expo = jnp.exp(scores - jnp.max(scores, axis=0, keepdims=True))
    total = jnp.sum(expo, axis=0, keepdims=True)
    share = jnp.transpose(jnp.broadcast_to(1.0 / total, (8, total.shape[1])))[:, :1]
    weights = expo.astype(jnp.bfloat16)
    width = 2 * head_count
    for start in range(0, weights.shape[1], width):
        mixed = product(weights[:, start : start + width], keys[:, :KV_RANK], ((0,), (0,)))
        mixed = mixed * share[start : start + width]
        yield mixed.astype(jnp.bfloat16).reshape(-1, head_count, KV_RANK)


def resident_kernel(length_ref, query_ref, step_ref, cache_ref, after_ref, out_ref, result, sem):
    result[...] = resident(length_ref[0], flat_rows(query_ref, 0), step_ref[0], cache_ref[0])
    copy = pltpu.make_async_copy(result, out_ref.at[0], sem)
    copy.start()
    copy.wait()


def middle_kernel(query_ref, step_ref, moved_ref, query_t_ref, tail_ref, *part_refs):
    decode = lax.axis_index("group") == 1

    @pl.when(decode)
    def _():
        query_t_ref[...] = jnp.transpose(flat_rows(query_ref, 1))
        tail_ref[...] = jnp.zeros_like(tail_ref)
        tail_ref[: step_ref.shape[1]] = step_ref[1]

    @pl.when(jnp.logical_not(decode))
    def _():
        count = moved_ref.shape[0] * moved_ref.shape[1]
        rows = lax.broadcasted_iota(jnp.int32, (count, count), 0)
        cols = lax.broadcasted_iota(jnp.int32, (count, count), 1)
        peer, part = rows % PEERS, rows // PEERS
        ahead = jnp.zeros_like(part)
        upper = lax.axis_index("z") == 1
        for index, (low_ahead, high_ahead) in enumerate(AHEAD):
            ahead = jnp.where(part == index, jnp.where(upper, high_ahead, low_ahead), ahead)
        moved = moved_ref[...].reshape(count, moved_ref.shape[2])
        turned = picked(cols == peer * LINE + ahead, moved, ((1,), (0,)))
        for part, part_ref in enumerate(part_refs):
            part_ref[...] = turned[part * PEERS : (part + 1) * PEERS]


def last_kernel(query_ref, step_ref, query_t_ref, tail_ref, *refs):
    part_refs, (out_ref, result, sems) = refs[:LINE], refs[LINE + 1 :]
    decode = lax.axis_index("group") == 1

    @pl.when(decode)
    def _():
        both = jnp.concatenate([ref[...] for ref in part_refs], axis=0)
        width = tail_ref.shape[1]
        keys = jnp.concatenate([both[:, :width], both[:, width:], tail_ref[...]], axis=0)
        base_count = keys.shape[0] - tail_ref.shape[0]
        copies = []
        for part, attended in enumerate(
            arrived_and_steps(query_t_ref[...], keys, base_count, query_ref.shape[2])
        ):
            steps = pl.ds(part * attended.shape[0], attended.shape[0])
            result[steps] = attended
            copies.append(
                pltpu.make_async_copy(result.at[steps], out_ref.at[1, steps], sems.at[part])
            )
            copies[-1].start()
        for copy in copies:
            copy.wait()

    @pl.when(jnp.logical_not(decode))
    def _():
        result[...] = steps_only(flat_rows(query_ref, 1), step_ref[1])
        copy = pltpu.make_async_copy(result, out_ref.at[1], sems.at[0])
        copy.start()
        copy.wait()


vmem = pl.BlockSpec(memory_space=pltpu.VMEM)
smem = pl.BlockSpec(memory_space=pltpu.SMEM)
anywhere = pl.BlockSpec(memory_space=pl.ANY)
params = pltpu.CompilerParams(vmem_limit_bytes=16 << 20)


def step_of(place, ahead):
    if ahead == LINE // 2:
        down = place % LINE >= LINE // 2 or place % 2 == 1
        return -ahead if down else ahead
    return ahead if ahead < LINE // 2 else ahead - LINE


def along_line(rows, index):
    line_total, ring = PEERS * LINE * 2, LINE * 2
    pairs = []
    for place in range(ring):
        for peer in range(PEERS):
            there = (place + step_of(place, AHEAD[index][peer // (PEERS // 2)])) % ring
            source = ((place % LINE) * PEERS + peer) * 2 + place // LINE
            target = ((there % LINE) * PEERS + peer) * 2 + there // LINE
            pairs.append((source, line_total + target))
    return lax.ppermute(rows, ("group", "pair", "z", "x", "y", "tp"), pairs)


def shards(queries, step_rows, cache, lengths, outgoing, crossing):
    seq_count, steps_total, head_count, latent_width = queries.shape
    row_total = outgoing.shape[0]
    first_shape = (steps_total, head_count, KV_RANK)
    keys = cache.transpose(0, 2, 1)

    query_rows = steps_total * head_count
    ahead = (crossing // PEERS - lax.axis_index("pair") + LINE) % LINE
    slots = (crossing % PEERS) * LINE + ahead
    mine = jnp.where(lax.axis_index("group") == 0, outgoing.T, jnp.zeros((), outgoing.dtype))
    packed = pl.pallas_call(
        pack_kernel,
        out_shape=jax.ShapeDtypeStruct((PEERS, LINE, 2 * latent_width), jnp.bfloat16),
        in_specs=[vmem] * 2,
        out_specs=vmem,
        compiler_params=params,
    )(slots.reshape(1, row_total), mine)
    moved = lax.cond(
        lax.axis_index("group") == 0,
        lambda rows: lax.all_to_all(rows, ("z", "x", "y"), 0, 0, tiled=True),
        jnp.zeros_like,
        packed,
    )
    query_t, tail, *parts = pl.pallas_call(
        middle_kernel,
        out_shape=[
            jax.ShapeDtypeStruct((latent_width, query_rows), jnp.bfloat16),
            jax.ShapeDtypeStruct((16, latent_width), jnp.bfloat16),
        ]
        + [jax.ShapeDtypeStruct((PEERS, 2 * latent_width), jnp.bfloat16)] * LINE,
        in_specs=[vmem] * 3,
        out_specs=[vmem] * (2 + LINE),
        compiler_params=params,
    )(queries, step_rows, moved)
    arrived = [along_line(part, index) for index, part in enumerate(parts)]
    out_shape = jax.ShapeDtypeStruct((seq_count,) + first_shape, jnp.bfloat16)
    half_done = pl.pallas_call(
        resident_kernel,
        out_shape=out_shape,
        in_specs=[smem] + [vmem] * 3 + [anywhere],
        out_specs=anywhere,
        scratch_shapes=[pltpu.VMEM(first_shape, jnp.bfloat16), pltpu.SemaphoreType.DMA],
        compiler_params=params,
    )(lengths, queries, step_rows, keys, tail)
    return pl.pallas_call(
        last_kernel,
        out_shape=out_shape,
        in_specs=[vmem] * (4 + LINE) + [anywhere],
        out_specs=anywhere,
        scratch_shapes=[pltpu.VMEM(first_shape, jnp.bfloat16), pltpu.SemaphoreType.DMA((2,))],
        input_output_aliases={4 + LINE: 0},
        compiler_params=params,
    )(queries, step_rows, query_t, tail, *arrived, half_done)


def solution(mesh):
    axes = ("group", "pair", "z", "x", "y", "tp")
    parted = Mesh(mesh.devices.reshape(2, LINE, 2, 4, 4, 2), axes)
    own = axes[:-1]
    placed = (
        P(own, None, "tp", None),
        P(own, None, None),
        P(own, None, None),
        P(own),
        P(own, None),
        P(own),
    )
    return jax.shard_map(
        shards,
        mesh=parted,
        in_specs=placed,
        out_specs=P(own, None, "tp", None),
        check_vma=False,
    )
```

```python
import jax
import jax.numpy as jnp
from jax import lax
from jax.experimental import pallas as pl
from jax.experimental.pallas import tpu as pltpu
from jax.sharding import Mesh, PartitionSpec as P

KV_RANK = 512
PEERS = 32
lap = 64
LINE = 4
AHEAD = ((1, 2), (2, 1), (3, 3), (0, 0))

score_scale = 192.0 ** (-0.5)
masked_score = -1e30


def product(left, right, dims):
    return lax.dot_general(left, right, (dims, ((), ())), preferred_element_type=jnp.float32)


def picked(where_one, rows, dims):
    selector = jnp.where(where_one, 1.0, 0.0).astype(jnp.bfloat16)
    return product(selector, rows, dims).astype(jnp.bfloat16)


def pack_kernel(slot_ref, latent_ref, packed_ref):
    width, count = latent_ref.shape
    each = count // 2
    rows = lax.broadcasted_iota(jnp.int32, (each, each), 0)
    blank = jnp.zeros((lap, each), latent_ref.dtype)
    first = picked(
        rows == slot_ref[:, :each], jnp.concatenate([latent_ref[:, :each], blank]), ((1,), (1,))
    )
    second = picked(
        rows == slot_ref[:, each:], jnp.concatenate([blank, latent_ref[:, each:]]), ((1,), (1,))
    )
    inner = width - lap
    both = jnp.concatenate(
        [first[:, :inner], first[:, inner:] + second[:, : 2 * lap], second[:, 2 * lap :]], axis=1
    )
    packed_ref[...] = both.reshape(packed_ref.shape)


def flat_rows(query_ref, seq):
    query = query_ref[seq]
    return query.reshape(query.shape[0] * query.shape[1], query.shape[2])


def step_scores(query, step_keys, head_count):
    scores = product(query, step_keys, ((1,), (1,))) * score_scale
    query_step = lax.broadcasted_iota(jnp.int32, scores.shape, 0) // head_count
    key_step = lax.broadcasted_iota(jnp.int32, scores.shape, 1)
    return jnp.where(key_step <= query_step, scores, masked_score)


def resident(length, query, step_keys, keys):
    head_count = query.shape[0] // step_keys.shape[0]
    scores = product(query, keys, ((1,), (0,))) * score_scale
    position = lax.broadcasted_iota(jnp.int32, scores.shape, 1)
    base_scores = jnp.where(position < length, scores, masked_score)
    tail_scores = step_scores(query, step_keys, head_count)
    peak = jnp.maximum(
        jnp.max(base_scores, axis=1, keepdims=True), jnp.max(tail_scores, axis=1, keepdims=True)
    )
    base_expo = jnp.exp(base_scores - peak)
    tail_expo = jnp.exp(tail_scores - peak)
    total = jnp.sum(base_expo, axis=1, keepdims=True) + jnp.sum(tail_expo, axis=1, keepdims=True)
    mixed = product(base_expo.astype(jnp.bfloat16), keys[:KV_RANK], ((1,), (1,))) + product(
        tail_expo.astype(jnp.bfloat16), step_keys[:, :KV_RANK], ((1,), (0,))
    )
    return (mixed * (1.0 / total)).astype(jnp.bfloat16).reshape(-1, head_count, KV_RANK)


def steps_only(query, step_keys):
    head_count = query.shape[0] // step_keys.shape[0]
    scores = step_scores(query, step_keys, head_count)
    expo = jnp.exp(scores - jnp.max(scores, axis=1, keepdims=True))
    total = jnp.sum(expo, axis=1, keepdims=True)
    mixed = product(expo.astype(jnp.bfloat16), step_keys[:, :KV_RANK], ((1,), (0,)))
    return (mixed * (1.0 / total)).astype(jnp.bfloat16).reshape(-1, head_count, KV_RANK)


def arrived_and_steps(query_t, keys, base_count, head_count):
    scores = product(keys, query_t, ((1,), (0,))) * score_scale
    step = lax.broadcasted_iota(jnp.int32, scores.shape, 0) - base_count
    query_step = lax.broadcasted_iota(jnp.int32, scores.shape, 1) // head_count
    scores = jnp.where(step <= query_step, scores, masked_score)
    expo = jnp.exp(scores - jnp.max(scores, axis=0, keepdims=True))
    total = jnp.sum(expo, axis=0, keepdims=True)
    share = jnp.transpose(jnp.broadcast_to(1.0 / total, (8, total.shape[1])))[:, :1]
    weights = expo.astype(jnp.bfloat16)
    width = 2 * head_count
    for start in range(0, weights.shape[1], width):
        mixed = product(weights[:, start : start + width], keys[:, :KV_RANK], ((0,), (0,)))
        mixed = mixed * share[start : start + width]
        yield mixed.astype(jnp.bfloat16).reshape(-1, head_count, KV_RANK)


def resident_kernel(length_ref, query_ref, step_ref, cache_ref, after_ref, out_ref, result, sem):
    result[...] = resident(length_ref[0], flat_rows(query_ref, 0), step_ref[0], cache_ref[0])
    copy = pltpu.make_async_copy(result, out_ref.at[0], sem)
    copy.start()
    copy.wait()


def middle_kernel(query_ref, step_ref, moved_ref, query_t_ref, tail_ref, *part_refs):
    decode = lax.axis_index("group") == 1

    @pl.when(decode)
    def _():
        query_t_ref[...] = jnp.transpose(flat_rows(query_ref, 1))
        tail_ref[...] = jnp.zeros_like(tail_ref)
        tail_ref[: step_ref.shape[1]] = step_ref[1]

    @pl.when(jnp.logical_not(decode))
    def _():
        count = moved_ref.shape[0] * moved_ref.shape[1]
        rows = lax.broadcasted_iota(jnp.int32, (count, count), 0)
        cols = lax.broadcasted_iota(jnp.int32, (count, count), 1)
        peer, part = rows % PEERS, rows // PEERS
        ahead = jnp.zeros_like(part)
        upper = lax.axis_index("z") == 1
        for index, (low_ahead, high_ahead) in enumerate(AHEAD):
            ahead = jnp.where(part == index, jnp.where(upper, high_ahead, low_ahead), ahead)
        moved = moved_ref[...].reshape(count, moved_ref.shape[2])
        turned = picked(cols == peer * LINE + ahead, moved, ((1,), (0,)))
        for part, part_ref in enumerate(part_refs):
            part_ref[...] = turned[part * PEERS : (part + 1) * PEERS]


def last_kernel(query_ref, step_ref, query_t_ref, tail_ref, *refs):
    part_refs, (out_ref, result, sems) = refs[:LINE], refs[LINE + 1 :]
    decode = lax.axis_index("group") == 1

    @pl.when(decode)
    def _():
        both = jnp.concatenate([ref[...] for ref in part_refs], axis=0)
        width = tail_ref.shape[1]
        keys = jnp.concatenate([both[:, :width], both[:, width:], tail_ref[...]], axis=0)
        base_count = keys.shape[0] - tail_ref.shape[0]
        copies = []
        for part, attended in enumerate(
            arrived_and_steps(query_t_ref[...], keys, base_count, query_ref.shape[2])
        ):
            steps = pl.ds(part * attended.shape[0], attended.shape[0])
            result[steps] = attended
            copies.append(
                pltpu.make_async_copy(result.at[steps], out_ref.at[1, steps], sems.at[part])
            )
            copies[-1].start()
        for copy in copies:
            copy.wait()

    @pl.when(jnp.logical_not(decode))
    def _():
        result[...] = steps_only(flat_rows(query_ref, 1), step_ref[1])
        copy = pltpu.make_async_copy(result, out_ref.at[1], sems.at[0])
        copy.start()
        copy.wait()


vmem = pl.BlockSpec(memory_space=pltpu.VMEM)
smem = pl.BlockSpec(memory_space=pltpu.SMEM)
anywhere = pl.BlockSpec(memory_space=pl.ANY)
params = pltpu.CompilerParams(vmem_limit_bytes=16 << 20)


def step_of(place, ahead):
    if ahead == LINE // 2:
        down = place % LINE >= LINE // 2 or place % 2 == 1
        return -ahead if down else ahead
    return ahead if ahead < LINE // 2 else ahead - LINE


def along_line(rows, index):
    line_total, ring = PEERS * LINE * 2, LINE * 2
    pairs = []
    for place in range(ring):
        for peer in range(PEERS):
            there = (place + step_of(place, AHEAD[index][peer // (PEERS // 2)])) % ring
            source = ((place % LINE) * PEERS + peer) * 2 + place // LINE
            target = ((there % LINE) * PEERS + peer) * 2 + there // LINE
            pairs.append((source, line_total + target))
    return lax.ppermute(rows, ("group", "pair", "z", "x", "y", "tp"), pairs)


def shards(queries, step_rows, cache, lengths, outgoing, crossing):
    seq_count, steps_total, head_count, latent_width = queries.shape
    row_total = outgoing.shape[0]
    first_shape = (steps_total, head_count, KV_RANK)
    keys = cache.transpose(0, 2, 1)

    query_rows = steps_total * head_count
    ahead = (crossing // PEERS - lax.axis_index("pair") + LINE) % LINE
    plane = PEERS // 2
    peer = (crossing % plane) * 2 + (crossing // plane) % 2
    slots = peer * LINE + ahead
    mine = jnp.where(lax.axis_index("group") == 0, outgoing.T, jnp.zeros((), outgoing.dtype))
    packed = pl.pallas_call(
        pack_kernel,
        out_shape=jax.ShapeDtypeStruct((PEERS, LINE, 2 * latent_width), jnp.bfloat16),
        in_specs=[vmem] * 2,
        out_specs=vmem,
        compiler_params=params,
    )(slots.reshape(1, row_total), mine)
    moved = lax.cond(
        lax.axis_index("group") == 0,
        lambda rows: lax.all_to_all(rows, ("x", "y", "z"), 0, 0, tiled=True),
        jnp.zeros_like,
        packed,
    )
    query_t, tail, *parts = pl.pallas_call(
        middle_kernel,
        out_shape=[
            jax.ShapeDtypeStruct((latent_width, query_rows), jnp.bfloat16),
            jax.ShapeDtypeStruct((16, latent_width), jnp.bfloat16),
        ]
        + [jax.ShapeDtypeStruct((PEERS, 2 * latent_width), jnp.bfloat16)] * LINE,
        in_specs=[vmem] * 3,
        out_specs=[vmem] * (2 + LINE),
        compiler_params=params,
    )(queries, step_rows, moved)
    arrived = [along_line(part, index) for index, part in enumerate(parts)]
    out_shape = jax.ShapeDtypeStruct((seq_count,) + first_shape, jnp.bfloat16)
    half_done = pl.pallas_call(
        resident_kernel,
        out_shape=out_shape,
        in_specs=[smem] + [vmem] * 3 + [anywhere],
        out_specs=anywhere,
        scratch_shapes=[pltpu.VMEM(first_shape, jnp.bfloat16), pltpu.SemaphoreType.DMA],
        compiler_params=params,
    )(lengths, queries, step_rows, keys, tail)
    return pl.pallas_call(
        last_kernel,
        out_shape=out_shape,
        in_specs=[vmem] * (4 + LINE) + [anywhere],
        out_specs=anywhere,
        scratch_shapes=[pltpu.VMEM(first_shape, jnp.bfloat16), pltpu.SemaphoreType.DMA((2,))],
        input_output_aliases={4 + LINE: 0},
        compiler_params=params,
    )(queries, step_rows, query_t, tail, *arrived, half_done)


def solution(mesh):
    axes = ("group", "pair", "z", "x", "y", "tp")
    parted = Mesh(mesh.devices.reshape(2, LINE, 2, 4, 4, 2), axes)
    own = axes[:-1]
    placed = (
        P(own, None, "tp", None),
        P(own, None, None),
        P(own, None, None),
        P(own),
        P(own, None),
        P(own),
    )
    return jax.shard_map(
        shards,
        mesh=parted,
        in_specs=placed,
        out_specs=P(own, None, "tp", None),
        check_vma=False,
    )
```

```python
import jax
import jax.numpy as jnp
from jax import lax
from jax.experimental import pallas as pl
from jax.experimental.pallas import tpu as pltpu
from jax.sharding import Mesh, PartitionSpec as P

KV_RANK = 512
PEERS = 32
lap = 64
LINE = 4
AHEAD = ((1, 2), (0, 1), (2, 3), (3, 0))

score_scale = 192.0 ** (-0.5)
masked_score = -1e30


def product(left, right, dims):
    return lax.dot_general(left, right, (dims, ((), ())), preferred_element_type=jnp.float32)


def picked(where_one, rows, dims):
    selector = jnp.where(where_one, 1.0, 0.0).astype(jnp.bfloat16)
    return product(selector, rows, dims).astype(jnp.bfloat16)


def pack_kernel(slot_ref, latent_ref, packed_ref):
    width, count = latent_ref.shape
    each = count // 2
    rows = lax.broadcasted_iota(jnp.int32, (each, each), 0)
    blank = jnp.zeros((lap, each), latent_ref.dtype)
    first = picked(
        rows == slot_ref[:, :each], jnp.concatenate([latent_ref[:, :each], blank]), ((1,), (1,))
    )
    second = picked(
        rows == slot_ref[:, each:], jnp.concatenate([blank, latent_ref[:, each:]]), ((1,), (1,))
    )
    inner = width - lap
    both = jnp.concatenate(
        [first[:, :inner], first[:, inner:] + second[:, : 2 * lap], second[:, 2 * lap :]], axis=1
    )
    packed_ref[...] = both.reshape(packed_ref.shape)


def flat_rows(query_ref, seq):
    query = query_ref[seq]
    return query.reshape(query.shape[0] * query.shape[1], query.shape[2])


def step_scores(query, step_keys, head_count):
    scores = product(query, step_keys, ((1,), (1,))) * score_scale
    query_step = lax.broadcasted_iota(jnp.int32, scores.shape, 0) // head_count
    key_step = lax.broadcasted_iota(jnp.int32, scores.shape, 1)
    return jnp.where(key_step <= query_step, scores, masked_score)


def resident(length, query, step_keys, keys):
    head_count = query.shape[0] // step_keys.shape[0]
    scores = product(query, keys, ((1,), (0,))) * score_scale
    position = lax.broadcasted_iota(jnp.int32, scores.shape, 1)
    base_scores = jnp.where(position < length, scores, masked_score)
    tail_scores = step_scores(query, step_keys, head_count)
    peak = jnp.maximum(
        jnp.max(base_scores, axis=1, keepdims=True), jnp.max(tail_scores, axis=1, keepdims=True)
    )
    base_expo = jnp.exp(base_scores - peak)
    tail_expo = jnp.exp(tail_scores - peak)
    total = jnp.sum(base_expo, axis=1, keepdims=True) + jnp.sum(tail_expo, axis=1, keepdims=True)
    mixed = product(base_expo.astype(jnp.bfloat16), keys[:KV_RANK], ((1,), (1,))) + product(
        tail_expo.astype(jnp.bfloat16), step_keys[:, :KV_RANK], ((1,), (0,))
    )
    return (mixed * (1.0 / total)).astype(jnp.bfloat16).reshape(-1, head_count, KV_RANK)


def steps_only(query, step_keys):
    head_count = query.shape[0] // step_keys.shape[0]
    scores = step_scores(query, step_keys, head_count)
    expo = jnp.exp(scores - jnp.max(scores, axis=1, keepdims=True))
    total = jnp.sum(expo, axis=1, keepdims=True)
    mixed = product(expo.astype(jnp.bfloat16), step_keys[:, :KV_RANK], ((1,), (0,)))
    return (mixed * (1.0 / total)).astype(jnp.bfloat16).reshape(-1, head_count, KV_RANK)


def arrived_and_steps(query_t, keys, base_count, head_count):
    scores = product(keys, query_t, ((1,), (0,))) * score_scale
    step = lax.broadcasted_iota(jnp.int32, scores.shape, 0) - base_count
    query_step = lax.broadcasted_iota(jnp.int32, scores.shape, 1) // head_count
    scores = jnp.where(step <= query_step, scores, masked_score)
    expo = jnp.exp(scores - jnp.max(scores, axis=0, keepdims=True))
    total = jnp.sum(expo, axis=0, keepdims=True)
    share = jnp.transpose(jnp.broadcast_to(1.0 / total, (8, total.shape[1])))[:, :1]
    weights = expo.astype(jnp.bfloat16)
    width = 2 * head_count
    for start in range(0, weights.shape[1], width):
        mixed = product(weights[:, start : start + width], keys[:, :KV_RANK], ((0,), (0,)))
        mixed = mixed * share[start : start + width]
        yield mixed.astype(jnp.bfloat16).reshape(-1, head_count, KV_RANK)


def resident_kernel(length_ref, query_ref, step_ref, cache_ref, after_ref, out_ref, result, sem):
    result[...] = resident(length_ref[0], flat_rows(query_ref, 0), step_ref[0], cache_ref[0])
    copy = pltpu.make_async_copy(result, out_ref.at[0], sem)
    copy.start()
    copy.wait()


def middle_kernel(query_ref, step_ref, moved_ref, query_t_ref, tail_ref, *part_refs):
    decode = lax.axis_index("group") == 1

    @pl.when(decode)
    def _():
        query_t_ref[...] = jnp.transpose(flat_rows(query_ref, 1))
        tail_ref[...] = jnp.zeros_like(tail_ref)
        tail_ref[: step_ref.shape[1]] = step_ref[1]

    @pl.when(jnp.logical_not(decode))
    def _():
        count = moved_ref.shape[0] * moved_ref.shape[1]
        rows = lax.broadcasted_iota(jnp.int32, (count, count), 0)
        cols = lax.broadcasted_iota(jnp.int32, (count, count), 1)
        peer, part = rows % PEERS, rows // PEERS
        ahead = jnp.zeros_like(part)
        upper = lax.axis_index("z") == 1
        for index, (low_ahead, high_ahead) in enumerate(AHEAD):
            ahead = jnp.where(part == index, jnp.where(upper, high_ahead, low_ahead), ahead)
        moved = moved_ref[...].reshape(count, moved_ref.shape[2])
        turned = picked(cols == peer * LINE + ahead, moved, ((1,), (0,)))
        for part, part_ref in enumerate(part_refs):
            part_ref[...] = turned[part * PEERS : (part + 1) * PEERS]


def last_kernel(query_ref, step_ref, query_t_ref, tail_ref, *refs):
    part_refs, (out_ref, result, sems) = refs[:LINE], refs[LINE + 1 :]
    decode = lax.axis_index("group") == 1

    @pl.when(decode)
    def _():
        both = jnp.concatenate([ref[...] for ref in part_refs], axis=0)
        width = tail_ref.shape[1]
        keys = jnp.concatenate([both[:, :width], both[:, width:], tail_ref[...]], axis=0)
        base_count = keys.shape[0] - tail_ref.shape[0]
        copies = []
        for part, attended in enumerate(
            arrived_and_steps(query_t_ref[...], keys, base_count, query_ref.shape[2])
        ):
            steps = pl.ds(part * attended.shape[0], attended.shape[0])
            result[steps] = attended
            copies.append(
                pltpu.make_async_copy(result.at[steps], out_ref.at[1, steps], sems.at[part])
            )
            copies[-1].start()
        for copy in copies:
            copy.wait()

    @pl.when(jnp.logical_not(decode))
    def _():
        result[...] = steps_only(flat_rows(query_ref, 1), step_ref[1])
        copy = pltpu.make_async_copy(result, out_ref.at[1], sems.at[0])
        copy.start()
        copy.wait()


vmem = pl.BlockSpec(memory_space=pltpu.VMEM)
smem = pl.BlockSpec(memory_space=pltpu.SMEM)
anywhere = pl.BlockSpec(memory_space=pl.ANY)
params = pltpu.CompilerParams(vmem_limit_bytes=16 << 20)


def step_of(place, ahead):
    if ahead == LINE // 2:
        down = place % LINE >= LINE // 2 or place % 2 == 1
        return -ahead if down else ahead
    return ahead if ahead < LINE // 2 else ahead - LINE


def along_line(rows, index):
    line_total, ring = PEERS * LINE * 2, LINE * 2
    pairs = []
    for place in range(ring):
        for peer in range(PEERS):
            there = (place + step_of(place, AHEAD[index][peer // (PEERS // 2)])) % ring
            source = ((place % LINE) * PEERS + peer) * 2 + place // LINE
            target = ((there % LINE) * PEERS + peer) * 2 + there // LINE
            pairs.append((source, line_total + target))
    return lax.ppermute(rows, ("group", "pair", "z", "x", "y", "tp"), pairs)


def shards(queries, step_rows, cache, lengths, outgoing, crossing):
    seq_count, steps_total, head_count, latent_width = queries.shape
    row_total = outgoing.shape[0]
    first_shape = (steps_total, head_count, KV_RANK)
    keys = cache.transpose(0, 2, 1)

    query_rows = steps_total * head_count
    ahead = (crossing // PEERS - lax.axis_index("pair") + LINE) % LINE
    slots = (crossing % PEERS) * LINE + ahead
    mine = jnp.where(lax.axis_index("group") == 0, outgoing.T, jnp.zeros((), outgoing.dtype))
    packed = pl.pallas_call(
        pack_kernel,
        out_shape=jax.ShapeDtypeStruct((PEERS, LINE, 2 * latent_width), jnp.bfloat16),
        in_specs=[vmem] * 2,
        out_specs=vmem,
        compiler_params=params,
    )(slots.reshape(1, row_total), mine)
    moved = lax.cond(
        lax.axis_index("group") == 0,
        lambda rows: lax.all_to_all(rows, ("z", "x", "y"), 0, 0, tiled=True),
        jnp.zeros_like,
        packed,
    )
    query_t, tail, *parts = pl.pallas_call(
        middle_kernel,
        out_shape=[
            jax.ShapeDtypeStruct((latent_width, query_rows), jnp.bfloat16),
            jax.ShapeDtypeStruct((16, latent_width), jnp.bfloat16),
        ]
        + [jax.ShapeDtypeStruct((PEERS, 2 * latent_width), jnp.bfloat16)] * LINE,
        in_specs=[vmem] * 3,
        out_specs=[vmem] * (2 + LINE),
        compiler_params=params,
    )(queries, step_rows, moved)
    arrived = [along_line(part, index) for index, part in enumerate(parts)]
    out_shape = jax.ShapeDtypeStruct((seq_count,) + first_shape, jnp.bfloat16)
    half_done = pl.pallas_call(
        resident_kernel,
        out_shape=out_shape,
        in_specs=[smem] + [vmem] * 3 + [anywhere],
        out_specs=anywhere,
        scratch_shapes=[pltpu.VMEM(first_shape, jnp.bfloat16), pltpu.SemaphoreType.DMA],
        compiler_params=params,
    )(lengths, queries, step_rows, keys, tail)
    return pl.pallas_call(
        last_kernel,
        out_shape=out_shape,
        in_specs=[vmem] * (4 + LINE) + [anywhere],
        out_specs=anywhere,
        scratch_shapes=[pltpu.VMEM(first_shape, jnp.bfloat16), pltpu.SemaphoreType.DMA((2,))],
        input_output_aliases={4 + LINE: 0},
        compiler_params=params,
    )(queries, step_rows, query_t, tail, *arrived, half_done)


def solution(mesh):
    axes = ("group", "pair", "z", "x", "y", "tp")
    parted = Mesh(mesh.devices.reshape(2, LINE, 2, 4, 4, 2), axes)
    own = axes[:-1]
    placed = (
        P(own, None, "tp", None),
        P(own, None, None),
        P(own, None, None),
        P(own),
        P(own, None),
        P(own),
    )
    return jax.shard_map(
        shards,
        mesh=parted,
        in_specs=placed,
        out_specs=P(own, None, "tp", None),
        check_vma=False,
    )
```

```python
import jax
import jax.numpy as jnp
from jax import lax
from jax.experimental import pallas as pl
from jax.experimental.pallas import tpu as pltpu
from jax.sharding import Mesh, PartitionSpec as P

KV_RANK = 512
PEERS = 32
lap = 64
LINE = 4
AHEAD = ((1, 2), (2, 1), (3, 3), (0, 0))

score_scale = 192.0 ** (-0.5)
masked_score = -1e30


def product(left, right, dims):
    return lax.dot_general(left, right, (dims, ((), ())), preferred_element_type=jnp.float32)


def picked(where_one, rows, dims):
    selector = jnp.where(where_one, 1.0, 0.0).astype(jnp.bfloat16)
    return product(selector, rows, dims).astype(jnp.bfloat16)


def pack_kernel(slot_ref, latent_ref, packed_ref):
    width, count = latent_ref.shape
    each = count // 2
    rows = lax.broadcasted_iota(jnp.int32, (each, each), 0)
    blank = jnp.zeros((lap, each), latent_ref.dtype)
    first = picked(
        rows == slot_ref[:, :each], jnp.concatenate([latent_ref[:, :each], blank]), ((1,), (1,))
    )
    second = picked(
        rows == slot_ref[:, each:], jnp.concatenate([blank, latent_ref[:, each:]]), ((1,), (1,))
    )
    inner = width - lap
    both = jnp.concatenate(
        [first[:, :inner], first[:, inner:] + second[:, : 2 * lap], second[:, 2 * lap :]], axis=1
    )
    packed_ref[...] = both.reshape(packed_ref.shape)


def flat_rows(query_ref, seq):
    query = query_ref[seq]
    return query.reshape(query.shape[0] * query.shape[1], query.shape[2])


def step_scores(query, step_keys, head_count):
    scores = product(query, step_keys, ((1,), (1,))) * score_scale
    query_step = lax.broadcasted_iota(jnp.int32, scores.shape, 0) // head_count
    key_step = lax.broadcasted_iota(jnp.int32, scores.shape, 1)
    return jnp.where(key_step <= query_step, scores, masked_score)


def resident(length, query, step_keys, keys):
    head_count = query.shape[0] // step_keys.shape[0]
    scores = product(query, keys, ((1,), (0,))) * score_scale
    position = lax.broadcasted_iota(jnp.int32, scores.shape, 1)
    base_scores = jnp.where(position < length, scores, masked_score)
    tail_scores = step_scores(query, step_keys, head_count)
    peak = jnp.maximum(
        jnp.max(base_scores, axis=1, keepdims=True), jnp.max(tail_scores, axis=1, keepdims=True)
    )
    base_expo = jnp.exp(base_scores - peak)
    tail_expo = jnp.exp(tail_scores - peak)
    total = jnp.sum(base_expo, axis=1, keepdims=True) + jnp.sum(tail_expo, axis=1, keepdims=True)
    mixed = product(base_expo.astype(jnp.bfloat16), keys[:KV_RANK], ((1,), (1,))) + product(
        tail_expo.astype(jnp.bfloat16), step_keys[:, :KV_RANK], ((1,), (0,))
    )
    return (mixed * (1.0 / total)).astype(jnp.bfloat16).reshape(-1, head_count, KV_RANK)


def steps_only(query, step_keys):
    head_count = query.shape[0] // step_keys.shape[0]
    scores = step_scores(query, step_keys, head_count)
    expo = jnp.exp(scores - jnp.max(scores, axis=1, keepdims=True))
    total = jnp.sum(expo, axis=1, keepdims=True)
    mixed = product(expo.astype(jnp.bfloat16), step_keys[:, :KV_RANK], ((1,), (0,)))
    return (mixed * (1.0 / total)).astype(jnp.bfloat16).reshape(-1, head_count, KV_RANK)


def arrived_and_steps(query_t, keys, base_count, head_count):
    scores = product(keys, query_t, ((1,), (0,))) * score_scale
    step = lax.broadcasted_iota(jnp.int32, scores.shape, 0) - base_count
    query_step = lax.broadcasted_iota(jnp.int32, scores.shape, 1) // head_count
    scores = jnp.where(step <= query_step, scores, masked_score)
    expo = jnp.exp(scores - jnp.max(scores, axis=0, keepdims=True))
    total = jnp.sum(expo, axis=0, keepdims=True)
    weights = expo.astype(jnp.bfloat16)
    step_count = query_t.shape[1] // head_count
    step_weights = weights[base_count:].astype(jnp.float32)[: 8 - 1]
    columns = jnp.transpose(jnp.concatenate([1.0 / total, step_weights], axis=0))
    step_values = keys[base_count:, :KV_RANK].astype(jnp.float32)
    width = 2 * head_count
    for start in range(0, weights.shape[1], width):
        own = columns[start : start + width]
        mixed = product(
            weights[:base_count, start : start + width], keys[:base_count, :KV_RANK], ((0,), (0,))
        )
        for index in range(step_count):
            mixed = mixed + own[:, 1 + index : 2 + index] * step_values[index : index + 1]
        mixed = mixed * own[:, :1]
        yield mixed.astype(jnp.bfloat16).reshape(-1, head_count, KV_RANK)


def resident_kernel(length_ref, query_ref, step_ref, cache_ref, after_ref, out_ref, result, sem):
    result[...] = resident(length_ref[0], flat_rows(query_ref, 0), step_ref[0], cache_ref[0])
    copy = pltpu.make_async_copy(result, out_ref.at[0], sem)
    copy.start()
    copy.wait()


def middle_kernel(query_ref, step_ref, moved_ref, query_t_ref, tail_ref, *part_refs):
    decode = lax.axis_index("group") == 1

    @pl.when(decode)
    def _():
        query_t_ref[...] = jnp.transpose(flat_rows(query_ref, 1))
        tail_ref[...] = jnp.zeros_like(tail_ref)
        tail_ref[: step_ref.shape[1]] = step_ref[1]

    @pl.when(jnp.logical_not(decode))
    def _():
        count = moved_ref.shape[0] * moved_ref.shape[1]
        rows = lax.broadcasted_iota(jnp.int32, (count, count), 0)
        cols = lax.broadcasted_iota(jnp.int32, (count, count), 1)
        peer, part = rows % PEERS, rows // PEERS
        ahead = jnp.zeros_like(part)
        upper = lax.axis_index("z") == 1
        for index, (low_ahead, high_ahead) in enumerate(AHEAD):
            ahead = jnp.where(part == index, jnp.where(upper, high_ahead, low_ahead), ahead)
        moved = moved_ref[...].reshape(count, moved_ref.shape[2])
        turned = picked(cols == peer * LINE + ahead, moved, ((1,), (0,)))
        for part, part_ref in enumerate(part_refs):
            part_ref[...] = turned[part * PEERS : (part + 1) * PEERS]


def last_kernel(query_ref, step_ref, query_t_ref, tail_ref, *refs):
    part_refs, (out_ref, result, sems) = refs[:LINE], refs[LINE + 1 :]
    decode = lax.axis_index("group") == 1

    @pl.when(decode)
    def _():
        both = jnp.concatenate([ref[...] for ref in part_refs], axis=0)
        width = tail_ref.shape[1]
        keys = jnp.concatenate([both[:, :width], both[:, width:], tail_ref[...]], axis=0)
        base_count = keys.shape[0] - tail_ref.shape[0]
        copies = []
        for part, attended in enumerate(
            arrived_and_steps(query_t_ref[...], keys, base_count, query_ref.shape[2])
        ):
            steps = pl.ds(part * attended.shape[0], attended.shape[0])
            result[steps] = attended
            copies.append(
                pltpu.make_async_copy(result.at[steps], out_ref.at[1, steps], sems.at[part])
            )
            copies[-1].start()
        for copy in copies:
            copy.wait()

    @pl.when(jnp.logical_not(decode))
    def _():
        result[...] = steps_only(flat_rows(query_ref, 1), step_ref[1])
        copy = pltpu.make_async_copy(result, out_ref.at[1], sems.at[0])
        copy.start()
        copy.wait()


vmem = pl.BlockSpec(memory_space=pltpu.VMEM)
smem = pl.BlockSpec(memory_space=pltpu.SMEM)
anywhere = pl.BlockSpec(memory_space=pl.ANY)
params = pltpu.CompilerParams(vmem_limit_bytes=16 << 20)


def step_of(place, ahead):
    if ahead == LINE // 2:
        down = place % LINE >= LINE // 2 or place % 2 == 1
        return -ahead if down else ahead
    return ahead if ahead < LINE // 2 else ahead - LINE


def along_line(rows, index):
    line_total, ring = PEERS * LINE * 2, LINE * 2
    pairs = []
    for place in range(ring):
        for peer in range(PEERS):
            there = (place + step_of(place, AHEAD[index][peer // (PEERS // 2)])) % ring
            source = ((place % LINE) * PEERS + peer) * 2 + place // LINE
            target = ((there % LINE) * PEERS + peer) * 2 + there // LINE
            pairs.append((source, line_total + target))
    return lax.ppermute(rows, ("group", "pair", "z", "x", "y", "tp"), pairs)


def shards(queries, step_rows, cache, lengths, outgoing, crossing):
    seq_count, steps_total, head_count, latent_width = queries.shape
    row_total = outgoing.shape[0]
    first_shape = (steps_total, head_count, KV_RANK)
    keys = cache.transpose(0, 2, 1)

    query_rows = steps_total * head_count
    ahead = (crossing // PEERS - lax.axis_index("pair") + LINE) % LINE
    slots = (crossing % PEERS) * LINE + ahead
    mine = jnp.where(lax.axis_index("group") == 0, outgoing.T, jnp.zeros((), outgoing.dtype))
    packed = pl.pallas_call(
        pack_kernel,
        out_shape=jax.ShapeDtypeStruct((PEERS, LINE, 2 * latent_width), jnp.bfloat16),
        in_specs=[vmem] * 2,
        out_specs=vmem,
        compiler_params=params,
    )(slots.reshape(1, row_total), mine)
    moved = lax.cond(
        lax.axis_index("group") == 0,
        lambda rows: lax.all_to_all(rows, ("z", "x", "y"), 0, 0, tiled=True),
        jnp.zeros_like,
        packed,
    )
    query_t, tail, *parts = pl.pallas_call(
        middle_kernel,
        out_shape=[
            jax.ShapeDtypeStruct((latent_width, query_rows), jnp.bfloat16),
            jax.ShapeDtypeStruct((16, latent_width), jnp.bfloat16),
        ]
        + [jax.ShapeDtypeStruct((PEERS, 2 * latent_width), jnp.bfloat16)] * LINE,
        in_specs=[vmem] * 3,
        out_specs=[vmem] * (2 + LINE),
        compiler_params=params,
    )(queries, step_rows, moved)
    arrived = [along_line(part, index) for index, part in enumerate(parts)]
    out_shape = jax.ShapeDtypeStruct((seq_count,) + first_shape, jnp.bfloat16)
    half_done = pl.pallas_call(
        resident_kernel,
        out_shape=out_shape,
        in_specs=[smem] + [vmem] * 3 + [anywhere],
        out_specs=anywhere,
        scratch_shapes=[pltpu.VMEM(first_shape, jnp.bfloat16), pltpu.SemaphoreType.DMA],
        compiler_params=params,
    )(lengths, queries, step_rows, keys, tail)
    return pl.pallas_call(
        last_kernel,
        out_shape=out_shape,
        in_specs=[vmem] * (4 + LINE) + [anywhere],
        out_specs=anywhere,
        scratch_shapes=[pltpu.VMEM(first_shape, jnp.bfloat16), pltpu.SemaphoreType.DMA((2,))],
        input_output_aliases={4 + LINE: 0},
        compiler_params=params,
    )(queries, step_rows, query_t, tail, *arrived, half_done)


def solution(mesh):
    axes = ("group", "pair", "z", "x", "y", "tp")
    parted = Mesh(mesh.devices.reshape(2, LINE, 2, 4, 4, 2), axes)
    own = axes[:-1]
    placed = (
        P(own, None, "tp", None),
        P(own, None, None),
        P(own, None, None),
        P(own),
        P(own, None),
        P(own),
    )
    return jax.shard_map(
        shards,
        mesh=parted,
        in_specs=placed,
        out_specs=P(own, None, "tp", None),
        check_vma=False,
    )
```
